256 devices in a mesh: band: 16 (over x, y), grow: 4 (over z_hi), gcol: 4 (over z_lo, core).
Axes of the slice: x: 4, y: 4, z: 8 (z_hi: 4, z_lo: 2; z = z_hi * 2 + z_lo), core: 2. Of those that a mesh axis runs over, the one named last changes fastest.
Arguments:
- valence: bfloat16 [4, 110592], replicated, may hold values from -6 to 6
- conduction: bfloat16 [256, 110592], P(('band', 'grow', 'gcol')), may hold values from -6 to 6
- val_energy: float32 [4], replicated, may hold values from -1 to 0
- cond_energy: float32 [256], replicated, may hold values from 0.2 to 3
- frequencies: float32 [2], replicated, may hold values from 0.1 to 2
- gvec_index: int32 [2048], replicated, may hold values from 0 to 110591, as said below
- first_band: int32 [4], replicated, may hold values from 0 to 127
Outputs:
- chi_zero: bfloat16 [2048, 2, 2, 2048], P(('grow', 'band'), None, None, 'gcol')
The draws below stay inside these ranges and needn't reach their ends.
Inputs may be any that keep to these rules, and one draw needn't show every extreme that they name: `gvec_index`: all 2048 entries are different.
All inputs are finite; a program needn't handle non-finite values.
Results may differ from the reference program's by a relative error of at most 0.0059.
Values may be sent and summed in bfloat16 or wider, within the bound.
No kernel may reach another device: no remote copies, remote signals or barrier semaphores. Data moves between devices by JAX's collectives and lax.ppermute only.
A program may use at most 128 MiB of HBM per device.

```python
import math
import jax
import jax.numpy as jnp
from jax import lax

NV = 4
GRID = 48
NGV = 2048
NW = 2
NC = 256


def draw_gvec_index(key, part):
    key = jax.random.fold_in(key, 1)
    first_key, second_key = jax.random.split(key)
    total = GRID ** 3
    inner = jax.random.permutation(first_key, total - 2)[:NGV - 2].astype(jnp.int32) + 1
    whole = jnp.concatenate([jnp.zeros((1,), jnp.int32), inner, jnp.full((1,), total - 1, jnp.int32)])
    return whole[jax.random.permutation(second_key, NGV)]


def draw_first_band(key, part):
    key = jax.random.fold_in(key, 2)
    first_key, second_key = jax.random.split(key)
    values = jax.random.randint(first_key, (NV,), 0, NC // 2).astype(jnp.int32)
    values = values.at[0].set(0).at[1].set(NC // 2 - 1)
    return values[jax.random.permutation(second_key, NV)]


def block_scale(key, extent, shards, low, high):
    def one(dim, blocks):
        steps = jax.random.uniform(jax.random.fold_in(jax.random.fold_in(key, 6), dim), (blocks,), jnp.float32, low / len(shards), high / len(shards))
        return jnp.repeat(jnp.exp(steps), extent[dim] // blocks).reshape((-1,) + (1,) * (len(extent) - dim - 1))

    gain = one(*shards[0])
    for cut in shards[1:]:
        gain = gain * one(*cut)
    return gain


def scatter_about(key, shape, scale, limit, cuts=(), kind=jnp.bfloat16):
    result = jax.random.normal(key, shape, jnp.float32) * scale
    if len(cuts) > 0:
        result = block_scale(key, shape, cuts, -0.22, 0.18) * result
    return jnp.clip(result, min=-limit, max=limit).astype(kind)


def setup_inputs(seed: int = 0) -> dict:
    splits = jax.random.split(jax.random.key(seed), 8)
    return {
        "valence": scatter_about(splits[0], (NV, GRID ** 3), 1.0, 6.0),
        "conduction": scatter_about(splits[1], (NC, GRID ** 3), 1.0, 6.0, ((0, 256),)),
        "val_energy": jnp.clip(jax.random.uniform(splits[2], (NV,), jnp.float32, -1.0, 0.0), -1.0, 0.0),
        "cond_energy": jnp.clip(jax.random.uniform(splits[3], (NC,), jnp.float32, 0.2, 3.0), 0.2, 3.0),
        "frequencies": jnp.clip(jnp.exp(jax.random.uniform(splits[4], (NW,), jnp.float32, math.log(0.1), math.log(2.0))), 0.1, 2.0),
        "gvec_index": draw_gvec_index(jax.random.fold_in(splits[7], 71), 0),
        "first_band": draw_first_band(jax.random.fold_in(splits[7], 71), 0),
    }


def reference(valence, conduction, val_energy, cond_energy, frequencies, gvec_index, first_band):
    points = GRID ** 3
    block = math.gcd(NC, 16)
    val_float = valence.astype(jnp.float32)

    def dens_block(cond_block):
        pair = cond_block.astype(jnp.float32)[:, None, :] * val_float[None]
        cube = pair.reshape(block, NV, GRID, GRID, GRID)
        spectrum = jnp.fft.fftn(cube, axes=(2, 3, 4)).reshape(block, NV, points) * (GRID ** -1.5)
        picked = spectrum[:, :, gvec_index]
        return jnp.stack([jnp.real(picked), jnp.imag(picked)], 1).astype(jnp.bfloat16)

    density = lax.map(dens_block, conduction.reshape(NC // block, block, points))
    density = density.reshape(NC, 2, NV, NGV)
    gap_value = cond_energy[None, :] - val_energy[:, None]
    counted = jnp.arange(NC, dtype=jnp.int32)[None, :] >= first_band[:, None]
    weight = jnp.where(counted[None], -4.0 * gap_value[None] / (gap_value[None] ** 2 + frequencies[:, None, None] ** 2), 0.0) / (NV * NC)
    dens_float = density.astype(jnp.float32)
    right_main = dens_float.reshape(NC * 2 * NV, NGV)
    right_swap = jnp.stack([-dens_float[:, 1], dens_float[:, 0]], 1).reshape(NC * 2 * NV, NGV)
    results = []
    for freq in range(NW):
        left = (jnp.transpose(weight[freq])[:, None, :, None] * dens_float).astype(jnp.bfloat16)
        left_mat = left.astype(jnp.float32).reshape(NC * 2 * NV, NGV)
        real_part = jnp.dot(left_mat.T, right_main, precision=lax.Precision.HIGHEST)
        imag_part = jnp.dot(left_mat.T, right_swap, precision=lax.Precision.HIGHEST)
        results.append(jnp.stack([real_part, imag_part], 1))
    return jnp.stack(results, 1).astype(jnp.bfloat16)
```

```python
import math

import jax
import jax.numpy as jnp
from jax import lax
from jax.sharding import Mesh, PartitionSpec as P

GRID = 48
ZED = ("grow", "zlo", "core")


def along_axis(spectrum, form, cos_one, sin_one):
    half = spectrum.shape[-1] // 2
    swapped = jnp.concatenate([spectrum[..., half:], -spectrum[..., :half]], -1)
    high = lax.Precision.HIGHEST
    return jnp.einsum(form, spectrum, cos_one, precision=high) + jnp.einsum(
        form, swapped, sin_one, precision=high
    )


def pair_density(valence, conduction, gvec_index):
    cond_count = conduction.shape[0]
    val_count = valence.shape[0]
    pairs = cond_count * val_count
    pair = conduction.astype(jnp.float32)[:, None, :] * valence.astype(jnp.float32)[None]
    flat_rows = pair.reshape(pairs * GRID * GRID, GRID)
    line = jnp.arange(GRID, dtype=jnp.int32)
    angle_one = 2.0 * math.pi * (line[:, None] * line[None, :] % GRID).astype(jnp.float32) / GRID
    cos_one = jnp.cos(angle_one)
    sin_one = jnp.sin(angle_one)
    first_table = jnp.concatenate([cos_one, -sin_one], 1)
    spectrum = jnp.dot(flat_rows, first_table, precision=lax.Precision.HIGHEST)
    spectrum = spectrum.reshape(pairs, GRID, GRID, 2 * GRID)
    spectrum = along_axis(spectrum, "pabz,bk->pakz", cos_one, sin_one)
    spectrum = along_axis(spectrum, "pabz,ak->pkbz", cos_one, sin_one)
    scale = GRID ** (-1.5)
    real_all = spectrum[..., :GRID].reshape(pairs, GRID**3) * scale
    imag_all = spectrum[..., GRID:].reshape(pairs, GRID**3) * scale
    real_pick = jnp.take(real_all, gvec_index, axis=1).reshape(cond_count, val_count, -1)
    imag_pick = jnp.take(imag_all, gvec_index, axis=1).reshape(cond_count, val_count, -1)
    return jnp.stack([real_pick, imag_pick], 1).astype(jnp.bfloat16)


def shift(array, axis, step):
    size = lax.axis_size(axis)
    return lax.ppermute(array, axis, [(k, (k + step) % size) for k in range(size)])


def weights(bands, val_energy, cond_energy, frequencies, first_band):
    energies = jnp.take(cond_energy, bands)
    gap = energies[:, None] - val_energy[None, :]
    counted = bands[:, None] >= first_band[None, :]
    total = cond_energy.shape[0] * val_energy.shape[0]
    ratio = -4.0 * gap[None] / (gap[None] ** 2 + frequencies[:, None, None] ** 2)
    return jnp.where(counted[None], ratio, 0.0) / total


def on_device(valence, conduction, val_energy, cond_energy, frequencies, gvec_index, first_band):
    density = pair_density(valence, conduction, gvec_index)
    num_gvec = density.shape[3]
    num_val = valence.shape[0]
    lines = 2 * num_val
    density = density.reshape(lines, num_gvec)
    rows_n = lax.axis_size("grow")
    cols_n = lax.axis_size("zlo") * lax.axis_size("core")
    across = lax.axis_size("bx")
    along = lax.axis_size("by")
    group = rows_n * cols_n
    col_tile = num_gvec // cols_n
    row_tile = num_gvec // rows_n
    row_part = row_tile // across
    by_col = jnp.transpose(density.reshape(lines, cols_n, col_tile), (1, 0, 2))
    by_row = jnp.transpose(density.reshape(lines, rows_n, row_tile), (1, 0, 2))
    sent = jnp.concatenate(
        [
            jnp.broadcast_to(by_col[None], (rows_n, cols_n, lines, col_tile)),
            jnp.broadcast_to(by_row[:, None], (rows_n, cols_n, lines, row_tile)),
        ],
        -1,
    ).reshape(group, lines, col_tile + row_tile)
    got = lax.all_to_all(sent, ZED, split_axis=0, concat_axis=0, tiled=True)
    got = got.reshape(group * lines, col_tile + row_tile)
    cols = got[:, :col_tile]
    rows = got[:, col_tile:]
    x_here = lax.axis_index("bx")
    y_here = lax.axis_index("by")
    parts = []
    for step in range(across):
        target = lax.rem(x_here + step, across)
        part = lax.dynamic_slice_in_dim(rows, target * row_part, row_part, 1)
        block = jnp.concatenate([cols, part], 1)
        parts.append(block if step == 0 else shift(block, "bx", step))
    whole = jnp.stack(parts)
    source = lax.rem(x_here - jnp.arange(across, dtype=jnp.int32) + across, across)
    bands = ((source * along + y_here) * group)[:, None] + jnp.arange(group, dtype=jnp.int32)
    weight = weights(bands.reshape(-1), val_energy, cond_energy, frequencies, first_band)
    right = whole[..., :col_tile].reshape(across * group * lines, col_tile)
    mine = whole[..., col_tile:].reshape(across * group, 2, num_val, row_part)
    left = (weight[:, :, None, :, None] * mine.astype(jnp.float32)[None]).astype(jnp.bfloat16)
    other = jnp.stack([left[:, :, 1], -left[:, :, 0]], 2)
    both = jnp.stack([left, other], 1)
    num_freq = frequencies.shape[0]
    both = both.reshape(num_freq, 2, across * group * lines, along, row_part // along)
    partial = jnp.einsum("wokyr,kh->yrwoh", both, right, preferred_element_type=jnp.float32)
    total = lax.dynamic_index_in_dim(partial, y_here, 0, keepdims=False)
    for step in range(1, along):
        target = lax.rem(y_here + step, along)
        piece = lax.dynamic_index_in_dim(partial, target, 0, keepdims=False)
        total = total + shift(piece.astype(jnp.bfloat16), "by", step).astype(jnp.float32)
    return total.astype(jnp.bfloat16)


def solution(mesh):
    fine = Mesh(mesh.devices.reshape(4, 4, 4, 2, 2), ("bx", "by", "grow", "zlo", "core"))
    return jax.shard_map(
        on_device,
        mesh=fine,
        in_specs=(P(), P(("bx", "by", "grow", "zlo", "core"), None), P(), P(), P(), P(), P()),
        out_specs=P(("grow", "bx", "by"), None, None, ("zlo", "core")),
        check_vma=False,
    )
```

```python
import numpy as np
import jax
import jax.numpy as jnp
from jax import lax
from jax.experimental import pallas as pl
from jax.experimental.pallas import tpu as pltpu
from jax.sharding import Mesh, PartitionSpec as P
import ml_dtypes

GRID = 48
HALF = GRID // 2 + 1
BF = jnp.bfloat16
ZED = ("grow", "zlo", "core")


def split_table(table):
    high = table.astype(ml_dtypes.bfloat16)
    low = (table - high.astype(np.float64)).astype(ml_dtypes.bfloat16)
    return high, low


def wave(left, right):
    angle = 2.0 * np.pi * (np.outer(left, right) % GRID) / GRID
    return np.cos(angle), np.sin(angle)


def tables():
    line = np.arange(GRID)
    cos, sin = wave(np.arange(HALF), line)
    first = np.zeros((2, HALF, 2, 4, 256))
    for odd in range(2):
        for b in range(4):
            at = 64 * odd + GRID * b
            first[odd, :, 0, b, at : at + GRID] = cos
            first[odd, :, 1, b, at : at + GRID] = -sin
    first = first.reshape(2, HALF * 8, 256)
    cos, sin = wave(line, line)
    order = np.zeros((2, GRID, 12, 2, 4))
    byb = cos.reshape(GRID, 12, 4)
    bys = sin.reshape(GRID, 12, 4)
    order[0, :, :, 0], order[0, :, :, 1] = byb, bys
    order[1, :, :, 0], order[1, :, :, 1] = -bys, byb
    second = order.reshape(2 * GRID, 2 * GRID)
    third = np.zeros((2, 2, GRID, 2, 128))
    for v in range(2):
        at = slice(GRID * v, GRID * v + GRID)
        third[v, 0, :, 0, at], third[v, 0, :, 1, at] = cos, sin
        third[v, 1, :, 0, at], third[v, 1, :, 1, at] = -sin, cos
    third = third.reshape(4 * GRID, 256)
    fh, fl = split_table(first)
    first = np.concatenate([fh, fl], 1)
    sh, sl = split_table(second)
    second = np.concatenate(
        [np.concatenate([sh, sh], 1), np.concatenate([sl, np.zeros_like(sl)], 1)], 0
    )
    th, tl = split_table(third)
    third = np.concatenate([th, tl], 0)
    return first, second, third


def dot_nt(a, b):
    return lax.dot_general(a, b, (((1,), (1,)), ((), ())), preferred_element_type=jnp.float32)


def dot_nn(a, b):
    return jnp.dot(a, b, preferred_element_type=jnp.float32)


def split(value):
    high = value.astype(BF)
    return high, (value - high.astype(jnp.float32)).astype(BF)


def density_kernel(cond, val, gvec, first, second, third, out, xh, xl, u, yh, yl, z, dens):
    zero = jnp.zeros((32, xh.shape[1]), BF)
    con = cond[...].astype(jnp.float32)
    for v in range(4):
        at = 128 * (v // 2) + GRID * (v % 2)
        high, low = split(con * val[v].astype(jnp.float32))
        xh[at : at + GRID, :] = high
        xl[at : at + GRID, :] = low
    for p in range(2):
        xh[128 * p + 96 : 128 * p + 128, :] = zero
        xl[128 * p + 96 : 128 * p + 128, :] = zero
    n1 = HALF * 8
    for pair in range(6):
        both = []
        for odd in range(2):
            start = 384 * pair + 128 * odd
            one = dot_nt(first[odd], xh[:, start : start + 256])
            two = dot_nt(first[odd, :n1], xl[:, start : start + 256])
            both.append((one[:n1] + one[n1:] + two).reshape(HALF, 8, 256))
        high, low = split(jnp.concatenate(both, 1))
        u[:, 16 * pair : 16 * pair + 16, :] = high
        u[:, 96 + 16 * pair : 96 + 16 * pair + 16, :] = low
    for k in range(HALF):
        full = dot_nn(second[...], u[k])
        high, low = split(full[:96] + full[96:])
        for p in range(2):
            for s in range(2):
                rows, lanes = slice(GRID * s, GRID * s + GRID), slice(128 * p, 128 * p + 128)
                put = (p, slice(GRID * k, GRID * k + GRID), slice(128 * s, 128 * s + 128))
                yh[put] = high[rows, lanes]
                yl[put] = low[rows, lanes]
    fill = yh.shape[1] - GRID * HALF
    blank = jnp.zeros((fill, 256), BF)
    for p in range(2):
        yh[p, GRID * HALF :, :] = blank
        yl[p, GRID * HALF :, :] = blank
        one = dot_nt(third[...], yh[p])
        two = dot_nt(third[:192], yl[p])
        z[192 * p : 192 * p + 192, :] = ((one[:192] + one[192:] + two) * GRID ** (-1.5)).astype(BF)
    for c in range(8):
        lanes = slice(256 * c, 256 * c + 256)
        g = gvec[:, lanes]
        plane = lax.shift_right_logical(lax.shift_right_logical(g, 4) * 43691, 17)
        k3 = g - plane * GRID
        k1 = lax.shift_right_logical(lax.shift_right_logical(plane, 4) * 43691, 17)
        k2 = plane - k1 * GRID
        flip = k3 >= HALF
        k1 = jnp.where(flip & (k1 > 0), GRID - k1, k1)
        k2 = jnp.where(flip & (k2 > 0), GRID - k2, k2)
        k3 = jnp.where(flip, GRID - k3, k3)
        spot = k3 * GRID + k2
        row = lax.broadcasted_iota(jnp.int32, (z.shape[1], 256), 0)
        hot = jnp.where(row == spot, 1.0, 0.0).astype(BF)
        t = dot_nn(z[...], hot)
        mask = lax.broadcasted_iota(jnp.int32, (GRID, 256), 0) == k1
        sign = jnp.where(flip, -1.0, 1.0)
        lines = []
        for s in range(2):
            for v in range(4):
                at = (2 * v + s) * GRID
                line = jnp.sum(jnp.where(mask, t[at : at + GRID], 0.0), 0, keepdims=True)
                lines.append(line * sign if s else line)
        dens[:, lanes] = jnp.concatenate(lines, 0)
    for i in range(4):
        for j in range(4):
            at = 16 * (4 * i + j)
            both = jnp.concatenate([dens[:, 512 * j : 512 * j + 512], dens[:, 512 * i : 512 * i + 512]], 0)
            out[at : at + 16, :] = both.astype(BF)


def density_call(valence, conduction, gvec_index):
    first, second, third = (jnp.asarray(t) for t in tables())
    cond = conduction.reshape(GRID, GRID * GRID)
    val = valence.reshape(4, GRID, GRID * GRID)
    gvec = gvec_index.reshape(1, -1)
    return pl.pallas_call(
        density_kernel,
        out_shape=jax.ShapeDtypeStruct((256, 512), BF),
        in_specs=[pl.BlockSpec(memory_space=pltpu.VMEM)] * 6,
        out_specs=pl.BlockSpec(memory_space=pltpu.VMEM),
        scratch_shapes=[
            pltpu.VMEM((256, 2304), BF),
            pltpu.VMEM((256, 2304), BF),
            pltpu.VMEM((HALF, 192, 256), BF),
            pltpu.VMEM((2, 1280, 256), BF),
            pltpu.VMEM((2, 1280, 256), BF),
            pltpu.VMEM((384, 1280), BF),
            pltpu.VMEM((8, 2048), jnp.float32),
        ],
        compiler_params=pltpu.CompilerParams(vmem_limit_bytes=48 * 1024 * 1024),
        cost_estimate=pl.CostEstimate(flops=5 * 10**9, bytes_accessed=3 * 10**6, transcendentals=0),
        name="density",
    )(cond, val, gvec, first, second, third)


def shift(array, axis, step):
    size = lax.axis_size(axis)
    return lax.ppermute(array, axis, [(k, (k + step) % size) for k in range(size)])


def weights(bands, val_energy, cond_energy, frequencies, first_band):
    energies = jnp.take(cond_energy, bands)
    gap = energies[:, None] - val_energy[None, :]
    counted = bands[:, None] >= first_band[None, :]
    total = cond_energy.shape[0] * val_energy.shape[0]
    ratio = -4.0 * gap[None] / (gap[None] ** 2 + frequencies[:, None, None] ** 2)
    return jnp.where(counted[None], ratio, 0.0) / total


def on_device(valence, conduction, val_energy, cond_energy, frequencies, gvec_index, first_band):
    sent = density_call(valence, conduction, gvec_index)
    num_gvec = gvec_index.shape[0]
    num_val = valence.shape[0]
    lines = 2 * num_val
    rows_n = lax.axis_size("grow")
    cols_n = lax.axis_size("zlo") * lax.axis_size("core")
    across = lax.axis_size("bx")
    along = lax.axis_size("by")
    group = rows_n * cols_n
    col_tile = num_gvec // cols_n
    row_tile = num_gvec // rows_n
    row_part = row_tile // across
    sent = sent.reshape(group, 2 * lines, col_tile)
    got = lax.all_to_all(sent, ZED, split_axis=0, concat_axis=0, tiled=True)
    cols = got[:, :lines].reshape(group * lines, col_tile)
    rows = got[:, lines:].reshape(group * lines, row_tile)
    x_here = lax.axis_index("bx")
    y_here = lax.axis_index("by")
    parts = []
    for step in range(across):
        target = lax.rem(x_here + step, across)
        part = lax.dynamic_slice_in_dim(rows, target * row_part, row_part, 1)
        block = jnp.concatenate([cols, part], 1)
        parts.append(block if step == 0 else shift(block, "bx", step))
    whole = jnp.stack(parts)
    source = lax.rem(x_here - jnp.arange(across, dtype=jnp.int32) + across, across)
    bands = ((source * along + y_here) * group)[:, None] + jnp.arange(group, dtype=jnp.int32)
    weight = weights(bands.reshape(-1), val_energy, cond_energy, frequencies, first_band)
    right = whole[..., :col_tile].reshape(across * group * lines, col_tile)
    mine = whole[..., col_tile:].reshape(across * group, 2, num_val, row_part)
    left = (weight[:, :, None, :, None] * mine.astype(jnp.float32)[None]).astype(jnp.bfloat16)
    other = jnp.stack([left[:, :, 1], -left[:, :, 0]], 2)
    both = jnp.stack([left, other], 1)
    num_freq = frequencies.shape[0]
    both = both.reshape(num_freq, 2, across * group * lines, along, row_part // along)
    partial = jnp.einsum("wokyr,kh->yrwoh", both, right, preferred_element_type=jnp.float32)
    total = lax.dynamic_index_in_dim(partial, y_here, 0, keepdims=False)
    for step in range(1, along):
        target = lax.rem(y_here + step, along)
        piece = lax.dynamic_index_in_dim(partial, target, 0, keepdims=False)
        total = total + shift(piece.astype(jnp.bfloat16), "by", step).astype(jnp.float32)
    return total.astype(jnp.bfloat16)


def solution(mesh):
    fine = Mesh(mesh.devices.reshape(4, 4, 4, 2, 2), ("bx", "by", "grow", "zlo", "core"))
    return jax.shard_map(
        on_device,
        mesh=fine,
        in_specs=(P(), P(("bx", "by", "grow", "zlo", "core"), None), P(), P(), P(), P(), P()),
        out_specs=P(("grow", "bx", "by"), None, None, ("zlo", "core")),
        check_vma=False,
    )
```

```python
import numpy as np
import jax
import jax.numpy as jnp
from jax import lax
from jax.experimental import pallas as pl
from jax.experimental.pallas import tpu as pltpu
from jax.sharding import Mesh, PartitionSpec as P
import ml_dtypes

GRID = 48
HALF = GRID // 2 + 1
BF = jnp.bfloat16
ZED = ("grow", "zlo", "core")
ALL = ("bx", "by") + ZED


def split_table(table):
    high = table.astype(ml_dtypes.bfloat16)
    low = (table - high.astype(np.float64)).astype(ml_dtypes.bfloat16)
    return high, low


def wave(left, right):
    angle = 2.0 * np.pi * (np.outer(left, right) % GRID) / GRID
    return np.cos(angle), np.sin(angle)


def tables():
    line = np.arange(GRID)
    cos, sin = wave(np.arange(HALF), line)
    first = np.zeros((2, HALF, 2, 4, 256))
    for odd in range(2):
        for b in range(4):
            at = 64 * odd + GRID * b
            first[odd, :, 0, b, at : at + GRID] = cos
            first[odd, :, 1, b, at : at + GRID] = -sin
    first = first.reshape(2, HALF * 8, 256)
    cos, sin = wave(line, line)
    order = np.zeros((2, GRID, 12, 2, 4))
    byb = cos.reshape(GRID, 12, 4)
    bys = sin.reshape(GRID, 12, 4)
    order[0, :, :, 0], order[0, :, :, 1] = byb, bys
    order[1, :, :, 0], order[1, :, :, 1] = -bys, byb
    second = order.reshape(2 * GRID, 2 * GRID)
    third = np.zeros((2, 2, GRID, 2, 128))
    for v in range(2):
        at = slice(GRID * v, GRID * v + GRID)
        third[v, 0, :, 0, at], third[v, 0, :, 1, at] = cos, sin
        third[v, 1, :, 0, at], third[v, 1, :, 1, at] = -sin, cos
    third = third.reshape(4 * GRID, 256)
    fh, fl = split_table(first)
    first = np.concatenate([fh, fl], 1)
    sh, sl = split_table(second)
    second = np.concatenate(
        [np.concatenate([sh, sh], 1), np.concatenate([sl, np.zeros_like(sl)], 1)], 0
    )
    th, tl = split_table(third)
    third = np.concatenate([th, tl], 0)
    return first, second, third


def dot_nt(a, b):
    return lax.dot_general(a, b, (((1,), (1,)), ((), ())), preferred_element_type=jnp.float32)


def dot_nn(a, b):
    return jnp.dot(a, b, preferred_element_type=jnp.float32)


def split(value):
    high = value.astype(BF)
    return high, (value - high.astype(jnp.float32)).astype(BF)


def density_kernel(cond, val, gvec, first, second, third, out, xh, xl, u, yh, yl, z, dens):
    zero = jnp.zeros((32, xh.shape[1]), BF)
    con = cond[0].astype(jnp.float32)
    for v in range(4):
        at = 128 * (v // 2) + GRID * (v % 2)
        high, low = split(con * val[v].astype(jnp.float32))
        xh[at : at + GRID, :] = high
        xl[at : at + GRID, :] = low
    for p in range(2):
        xh[128 * p + 96 : 128 * p + 128, :] = zero
        xl[128 * p + 96 : 128 * p + 128, :] = zero
    n1 = HALF * 8
    for pair in range(6):
        both = []
        for odd in range(2):
            start = 384 * pair + 128 * odd
            one = dot_nt(first[odd], xh[:, start : start + 256])
            two = dot_nt(first[odd, :n1], xl[:, start : start + 256])
            both.append((one[:n1] + one[n1:] + two).reshape(HALF, 8, 256))
        high, low = split(jnp.concatenate(both, 1))
        u[:, 16 * pair : 16 * pair + 16, :] = high
        u[:, 96 + 16 * pair : 96 + 16 * pair + 16, :] = low
    for k in range(HALF):
        full = dot_nn(second[...], u[k])
        high, low = split(full[:96] + full[96:])
        for p in range(2):
            for s in range(2):
                rows, lanes = slice(GRID * s, GRID * s + GRID), slice(128 * p, 128 * p + 128)
                put = (p, slice(GRID * k, GRID * k + GRID), slice(128 * s, 128 * s + 128))
                yh[put] = high[rows, lanes]
                yl[put] = low[rows, lanes]
    fill = yh.shape[1] - GRID * HALF
    blank = jnp.zeros((fill, 256), BF)
    for p in range(2):
        yh[p, GRID * HALF :, :] = blank
        yl[p, GRID * HALF :, :] = blank
        one = dot_nt(third[...], yh[p])
        two = dot_nt(third[:192], yl[p])
        z[192 * p : 192 * p + 192, :] = ((one[:192] + one[192:] + two) * GRID ** (-1.5)).astype(BF)
    for c in range(8):
        lanes = slice(256 * c, 256 * c + 256)
        g = gvec[:, lanes]
        plane = lax.shift_right_logical(lax.shift_right_logical(g, 4) * 43691, 17)
        k3 = g - plane * GRID
        k1 = lax.shift_right_logical(lax.shift_right_logical(plane, 4) * 43691, 17)
        k2 = plane - k1 * GRID
        flip = k3 >= HALF
        k1 = jnp.where(flip & (k1 > 0), GRID - k1, k1)
        k2 = jnp.where(flip & (k2 > 0), GRID - k2, k2)
        k3 = jnp.where(flip, GRID - k3, k3)
        spot = k3 * GRID + k2
        row = lax.broadcasted_iota(jnp.int32, (z.shape[1], 256), 0)
        hot = jnp.where(row == spot, 1.0, 0.0).astype(BF)
        t = dot_nn(z[...], hot)
        mask = lax.broadcasted_iota(jnp.int32, (GRID, 256), 0) == k1
        sign = jnp.where(flip, -1.0, 1.0)
        lines = []
        for s in range(2):
            for v in range(4):
                at = (2 * v + s) * GRID
                line = jnp.sum(jnp.where(mask, t[at : at + GRID], 0.0), 0, keepdims=True)
                lines.append(line * sign if s else line)
        dens[:, lanes] = jnp.concatenate(lines, 0)
    quarter = lax.broadcasted_iota(jnp.int32, (8, 128), 1) // 32
    for i in range(4):
        tiles = [dens[:, 512 * i + 128 * t : 512 * i + 128 * t + 128] for t in range(4)]
        turned = []
        for t in range(4):
            tile = tiles[t]
            for other in range(4):
                if other != t:
                    moved = pltpu.roll(tiles[other], (32 * (other - t)) % 128, 1)
                    tile = jnp.where(quarter == other, moved, tile)
            turned.append(tile)
        orders = (jnp.concatenate(tiles, 1), jnp.concatenate(turned, 1))
        for j in range(4):
            at = 16 * (4 * i + j)
            both = jnp.concatenate([dens[:, 512 * j : 512 * j + 512], orders[j % 2]], 0)
            out[at : at + 16, :] = both.astype(BF)


def density_call(valence, conduction, gvec_index):
    first, second, third = (jnp.asarray(t) for t in tables())
    cond = jnp.pad(conduction, ((0, 3), (0, 0))).reshape(4, GRID, GRID * GRID)
    val = valence.reshape(4, GRID, GRID * GRID)
    gvec = gvec_index.reshape(1, -1)
    return pl.pallas_call(
        density_kernel,
        out_shape=jax.ShapeDtypeStruct((256, 512), BF),
        in_specs=[pl.BlockSpec(memory_space=pltpu.VMEM)] * 6,
        out_specs=pl.BlockSpec(memory_space=pltpu.VMEM),
        scratch_shapes=[
            pltpu.VMEM((256, 2304), BF),
            pltpu.VMEM((256, 2304), BF),
            pltpu.VMEM((HALF, 192, 256), BF),
            pltpu.VMEM((2, 1280, 256), BF),
            pltpu.VMEM((2, 1280, 256), BF),
            pltpu.VMEM((384, 1280), BF),
            pltpu.VMEM((8, 2048), jnp.float32),
        ],
        compiler_params=pltpu.CompilerParams(vmem_limit_bytes=48 * 1024 * 1024),
        cost_estimate=pl.CostEstimate(flops=5 * 10**9, bytes_accessed=3 * 10**6, transcendentals=0),
        name="density",
    )(cond, val, gvec, first, second, third)


def product_kernel(turn, weight, own, one, two, three, mine, first, second, third):
    cols, lefts = [], []
    for n, block in enumerate((own, one, two, three)):
        cols.append(block[:, :512])
        rows = block[:, 512:640].astype(jnp.float32)
        rows = pltpu.roll(rows, lax.rem(128 - 32 * turn[0], 128), 1)
        split_rows = rows.reshape(16, 2, 4, 128)
        swapped = jnp.concatenate([split_rows[:, 1:], -split_rows[:, :1]], 1).reshape(128, 128)
        parts = []
        for freq in range(2):
            scale = weight[n, :, freq : freq + 1]
            parts.append((scale * rows).astype(BF))
            parts.append((scale * swapped).astype(BF))
        lefts.append(jnp.concatenate(parts, 1))
    left = jnp.concatenate(lefts, 0)
    right = jnp.concatenate(cols, 0)
    total = lax.dot_general(left, right, (((0,), (0,)), ((), ())), preferred_element_type=jnp.float32)
    for part in range(4):
        at = 128 * part
        mine[32 * part : 32 * part + 32, :] = total[at : at + 32]
        first[32 * part : 32 * part + 32, :] = total[at + 32 : at + 64].astype(BF)
        second[32 * part : 32 * part + 32, :] = total[at + 64 : at + 96].astype(BF)
        third[32 * part : 32 * part + 32, :] = total[at + 96 : at + 128].astype(BF)


def product_call(turn, weight, blocks):
    piece = jax.ShapeDtypeStruct((128, 512), BF)
    vmem = pl.BlockSpec(memory_space=pltpu.VMEM)
    return pl.pallas_call(
        product_kernel,
        out_shape=(jax.ShapeDtypeStruct((128, 512), jnp.float32), piece, piece, piece),
        in_specs=[pl.BlockSpec(memory_space=pltpu.SMEM)] + [vmem] * 5,
        out_specs=(vmem,) * 4,
        compiler_params=pltpu.CompilerParams(vmem_limit_bytes=48 * 1024 * 1024),
        cost_estimate=pl.CostEstimate(flops=3 * 10**8, bytes_accessed=2 * 10**6, transcendentals=0),
        name="product",
    )(turn, weight, *blocks)


def ring_pairs(across, along, rest, step, gather):
    pairs = []
    for x in range(across):
        for y in range(along):
            for z in range(rest):
                if (z % 2 == 0) == gather:
                    to = ((x + step) % across, y)
                else:
                    to = (x, (y + step) % along)
                pairs.append(((x * along + y) * rest + z, (to[0] * along + to[1]) * rest + z))
    return pairs


def on_device(valence, conduction, val_energy, cond_energy, frequencies, gvec_index, first_band):
    sent = density_call(valence, conduction, gvec_index)
    num_val = valence.shape[0]
    lines = 2 * num_val
    across = lax.axis_size("bx")
    along = lax.axis_size("by")
    group = lax.axis_size("grow") * lax.axis_size("zlo") * lax.axis_size("core")
    sent = sent.reshape(group, 2 * lines, 512)
    got = lax.all_to_all(sent, ZED, split_axis=0, concat_axis=0, tiled=True)
    cols = got[:, :lines].reshape(group * lines, 512)
    rows = got[:, lines:].reshape(group * lines, 512)
    x_here = lax.axis_index("bx")
    y_here = lax.axis_index("by")
    even = lax.axis_index("core") == 0
    place = jnp.where(even, x_here, y_here)
    other = jnp.where(even, y_here, x_here)
    blocks = {}
    for step in (0, 1, 3, 2):
        target = lax.rem(place + step, across)
        part = lax.dynamic_slice_in_dim(rows, target * 128, 128, 1)
        block = jnp.concatenate([cols, part], 1)
        pairs = ring_pairs(across, along, group, step, True)
        blocks[step] = lax.ppermute(block, ALL, pairs) if step else block
    source = lax.rem(place - jnp.arange(across, dtype=jnp.int32) + across, across)
    band = jnp.where(even, source * along + other, other * along + source)
    bands = (band * group)[:, None] + jnp.arange(group, dtype=jnp.int32)
    energies = jnp.take(cond_energy, bands)
    gap = energies[..., None] - val_energy
    counted = bands[..., None] >= first_band
    ratio = -4.0 * gap[..., None] / (gap[..., None] ** 2 + frequencies**2)
    weight = jnp.where(counted[..., None], ratio, 0.0) / (cond_energy.shape[0] * num_val)
    weight = jnp.broadcast_to(weight[:, :, None], (across, group, 2, num_val, frequencies.shape[0]))
    weight = weight.reshape(across, group * lines, frequencies.shape[0])
    total, *pieces = product_call(other.reshape(1), weight, [blocks[step] for step in range(across)])
    for step in (1, 3, 2):
        pairs = ring_pairs(across, along, group, step, False)
        total = total + lax.ppermute(pieces[step - 1], ALL, pairs).astype(jnp.float32)
    return jnp.transpose(total.reshape(2, 2, 32, 512), (2, 0, 1, 3)).astype(BF)


def solution(mesh):
    fine = Mesh(mesh.devices.reshape(4, 4, 4, 2, 2), ALL)
    return jax.shard_map(
        on_device,
        mesh=fine,
        in_specs=(P(), P(ALL, None), P(), P(), P(), P(), P()),
        out_specs=P(("grow", "bx", "by"), None, None, ("zlo", "core")),
        check_vma=False,
    )
```

```python
import numpy as np
import jax
import jax.numpy as jnp
from jax import lax
from jax.experimental import pallas as pl
from jax.experimental.pallas import tpu as pltpu
from jax.sharding import Mesh, PartitionSpec as P
import ml_dtypes

GRID = 48
HALF = GRID // 2 + 1
BF = jnp.bfloat16
ZED = ("grow", "zlo", "core")
ALL = ("bx", "by") + ZED


def split_table(table):
    high = table.astype(ml_dtypes.bfloat16)
    low = (table - high.astype(np.float64)).astype(ml_dtypes.bfloat16)
    return high, low


def wave(left, right):
    angle = 2.0 * np.pi * (np.outer(left, right) % GRID) / GRID
    return np.cos(angle), np.sin(angle)


def tables():
    line = np.arange(GRID)
    cos, sin = wave(np.arange(HALF), line)
    first = np.zeros((2, HALF, 2, 4, 256))
    for odd in range(2):
        for b in range(4):
            at = 64 * odd + GRID * b
            first[odd, :, 0, b, at : at + GRID] = cos
            first[odd, :, 1, b, at : at + GRID] = -sin
    first = first.reshape(2, HALF * 8, 256)
    cos, sin = wave(line, line)
    order = np.zeros((2, GRID, 12, 2, 4))
    byb = cos.reshape(GRID, 12, 4)
    bys = sin.reshape(GRID, 12, 4)
    order[0, :, :, 0], order[0, :, :, 1] = byb, bys
    order[1, :, :, 0], order[1, :, :, 1] = -bys, byb
    second = order.reshape(2 * GRID, 2 * GRID)
    third = np.zeros((2, 2, GRID, 2, 128))
    for v in range(2):
        at = slice(GRID * v, GRID * v + GRID)
        third[v, 0, :, 0, at], third[v, 0, :, 1, at] = cos, sin
        third[v, 1, :, 0, at], third[v, 1, :, 1, at] = -sin, cos
    third = third.reshape(4 * GRID, 256)
    fh, fl = split_table(first)
    first = np.concatenate([fh, fl], 1)
    sh, sl = split_table(second)
    second = np.concatenate(
        [np.concatenate([sh, sh], 1), np.concatenate([sl, np.zeros_like(sl)], 1)], 0
    )
    th, tl = split_table(third)
    third = np.concatenate([th, tl], 0)
    return first, second, third


def dot_nt(a, b):
    return lax.dot_general(a, b, (((1,), (1,)), ((), ())), preferred_element_type=jnp.float32)


def dot_nn(a, b):
    return jnp.dot(a, b, preferred_element_type=jnp.float32)


def split(value):
    high = value.astype(BF)
    return high, (value - high.astype(jnp.float32)).astype(BF)


MEMBERS = (((0, 1), (2, 3)), ((0, 3), (1, 2)))


def reduce_order(tiles, quarter, kind):
    result = []
    for xs in MEMBERS[kind]:
        for ys in MEMBERS[kind]:
            made = None
            for n in range(4):
                x, y = xs[n // 2], ys[n % 2]
                shift = 32 * (n - y) % 128
                moved = pltpu.roll(tiles[x], shift, 1) if shift else tiles[x]
                made = moved if made is None else jnp.where(quarter == n, moved, made)
            result.append(made)
    return jnp.concatenate(result, 1)


def density_kernel(cond, val, gvec, first, second, third, out, xh, xl, u, yh, yl, z, dens):
    zero = jnp.zeros((32, xh.shape[1]), BF)
    con = cond[0].astype(jnp.float32)
    for v in range(4):
        at = 128 * (v // 2) + GRID * (v % 2)
        high, low = split(con * val[v].astype(jnp.float32))
        xh[at : at + GRID, :] = high
        xl[at : at + GRID, :] = low
    for p in range(2):
        xh[128 * p + 96 : 128 * p + 128, :] = zero
        xl[128 * p + 96 : 128 * p + 128, :] = zero
    n1 = HALF * 8
    for pair in range(6):
        both = []
        for odd in range(2):
            start = 384 * pair + 128 * odd
            one = dot_nt(first[odd], xh[:, start : start + 256])
            two = dot_nt(first[odd, :n1], xl[:, start : start + 256])
            both.append((one[:n1] + one[n1:] + two).reshape(HALF, 8, 256))
        high, low = split(jnp.concatenate(both, 1))
        u[:, 16 * pair : 16 * pair + 16, :] = high
        u[:, 96 + 16 * pair : 96 + 16 * pair + 16, :] = low
    for k in range(HALF):
        full = dot_nn(second[...], u[k])
        high, low = split(full[:96] + full[96:])
        for p in range(2):
            for s in range(2):
                rows, lanes = slice(GRID * s, GRID * s + GRID), slice(128 * p, 128 * p + 128)
                put = (p, slice(GRID * k, GRID * k + GRID), slice(128 * s, 128 * s + 128))
                yh[put] = high[rows, lanes]
                yl[put] = low[rows, lanes]
    fill = yh.shape[1] - GRID * HALF
    blank = jnp.zeros((fill, 256), BF)
    for p in range(2):
        yh[p, GRID * HALF :, :] = blank
        yl[p, GRID * HALF :, :] = blank
        one = dot_nt(third[...], yh[p])
        two = dot_nt(third[:192], yl[p])
        z[192 * p : 192 * p + 192, :] = ((one[:192] + one[192:] + two) * GRID ** (-1.5)).astype(BF)
    for c in range(8):
        lanes = slice(256 * c, 256 * c + 256)
        g = gvec[:, lanes]
        plane = lax.shift_right_logical(lax.shift_right_logical(g, 4) * 43691, 17)
        k3 = g - plane * GRID
        k1 = lax.shift_right_logical(lax.shift_right_logical(plane, 4) * 43691, 17)
        k2 = plane - k1 * GRID
        flip = k3 >= HALF
        k1 = jnp.where(flip & (k1 > 0), GRID - k1, k1)
        k2 = jnp.where(flip & (k2 > 0), GRID - k2, k2)
        k3 = jnp.where(flip, GRID - k3, k3)
        spot = k3 * GRID + k2
        row = lax.broadcasted_iota(jnp.int32, (z.shape[1], 256), 0)
        hot = jnp.where(row == spot, 1.0, 0.0).astype(BF)
        t = dot_nn(z[...], hot)
        mask = lax.broadcasted_iota(jnp.int32, (GRID, 256), 0) == k1
        sign = jnp.where(flip, -1.0, 1.0)
        lines = []
        for s in range(2):
            for v in range(4):
                at = (2 * v + s) * GRID
                line = jnp.sum(jnp.where(mask, t[at : at + GRID], 0.0), 0, keepdims=True)
                lines.append(line * sign if s else line)
        dens[:, lanes] = jnp.concatenate(lines, 0)
    quarter = lax.broadcasted_iota(jnp.int32, (8, 128), 1) // 32
    for i in range(4):
        tiles = [dens[:, 512 * i + 128 * t : 512 * i + 128 * t + 128] for t in range(4)]
        orders = [reduce_order(tiles, quarter, kind) for kind in (1, 0)]
        for j in range(4):
            at = 16 * (4 * i + j)
            both = jnp.concatenate([dens[:, 512 * j : 512 * j + 512], orders[j % 2]], 0)
            out[at : at + 16, :] = both.astype(BF)


def density_call(valence, conduction, gvec_index):
    first, second, third = (jnp.asarray(t) for t in tables())
    cond = jnp.pad(conduction, ((0, 3), (0, 0))).reshape(4, GRID, GRID * GRID)
    val = valence.reshape(4, GRID, GRID * GRID)
    gvec = gvec_index.reshape(1, -1)
    return pl.pallas_call(
        density_kernel,
        out_shape=jax.ShapeDtypeStruct((256, 512), BF),
        in_specs=[pl.BlockSpec(memory_space=pltpu.VMEM)] * 6,
        out_specs=pl.BlockSpec(memory_space=pltpu.VMEM),
        scratch_shapes=[
            pltpu.VMEM((256, 2304), BF),
            pltpu.VMEM((256, 2304), BF),
            pltpu.VMEM((HALF, 192, 256), BF),
            pltpu.VMEM((2, 1280, 256), BF),
            pltpu.VMEM((2, 1280, 256), BF),
            pltpu.VMEM((384, 1280), BF),
            pltpu.VMEM((8, 2048), jnp.float32),
        ],
        compiler_params=pltpu.CompilerParams(vmem_limit_bytes=48 * 1024 * 1024),
        cost_estimate=pl.CostEstimate(flops=5 * 10**9, bytes_accessed=3 * 10**6, transcendentals=0),
        name="density",
    )(cond, val, gvec, first, second, third)


def product_kernel(turn, weight, own, one, two, three, mine, first, second, third):
    blocks = (own, one, two, three)
    twice = []
    for block in blocks:
        rows = block[:, 512:640]
        parts = rows.astype(jnp.float32).reshape(16, 2, 4, 128)
        swapped = jnp.concatenate([parts[:, 1:], -parts[:, :1]], 1).reshape(128, 128)
        twice.append(jnp.concatenate([rows, swapped.astype(BF)], 1))
    lane = lax.broadcasted_iota(jnp.int32, (256, 512), 1)
    spot = ((lane // 128) ^ turn[0]) * 32 + (lane // 4) % 32 + 128 * (lane % 2)
    copies = jnp.where(lax.broadcasted_iota(jnp.int32, (256, 512), 0) == spot, 1.0, 0.0).astype(BF)
    spread = dot_nn(jnp.concatenate(twice, 0), copies)
    scale = weight[...].reshape(512, 2)
    early = (lax.broadcasted_iota(jnp.int32, (512, 512), 1) // 2) % 2 == 0
    left = (jnp.where(early, scale[:, 0:1], scale[:, 1:2]) * spread).astype(BF)
    right = jnp.concatenate([block[:, :512] for block in blocks], 0)
    total = lax.dot_general(left, right, (((0,), (0,)), ((), ())), preferred_element_type=jnp.float32)
    mine[...] = total[:128]
    first[...] = total[128:256].astype(BF)
    second[...] = total[256:384].astype(BF)
    third[...] = total[384:].astype(BF)


def product_call(turn, weight, blocks):
    piece = jax.ShapeDtypeStruct((128, 512), BF)
    vmem = pl.BlockSpec(memory_space=pltpu.VMEM)
    return pl.pallas_call(
        product_kernel,
        out_shape=(jax.ShapeDtypeStruct((128, 512), jnp.float32), piece, piece, piece),
        in_specs=[pl.BlockSpec(memory_space=pltpu.SMEM)] + [vmem] * 5,
        out_specs=(vmem,) * 4,
        compiler_params=pltpu.CompilerParams(vmem_limit_bytes=48 * 1024 * 1024),
        cost_estimate=pl.CostEstimate(flops=3 * 10**8, bytes_accessed=2 * 10**6, transcendentals=0),
        name="product",
    )(turn, weight, *blocks)


def sum_kernel(mine, first, second, third, out):
    total = mine[...]
    for piece in (first, second, third):
        total = total + piece[...].astype(jnp.float32)
    out[...] = total.reshape(out.shape).astype(BF)


def sum_call(mine, pieces, shape):
    vmem = pl.BlockSpec(memory_space=pltpu.VMEM)
    return pl.pallas_call(
        sum_kernel,
        out_shape=jax.ShapeDtypeStruct(shape, BF),
        in_specs=[vmem] * 4,
        out_specs=vmem,
        name="add",
    )(mine, *pieces)


def exchange(block, step, gather):
    across, along = lax.axis_size("bx"), lax.axis_size("by")
    rest = lax.axis_size("grow") * lax.axis_size("zlo") * lax.axis_size("core")

    def partner(place, kind):
        return 3 - place if kind else place ^ 1

    pairs = []
    for x in range(across):
        for y in range(along):
            for z in range(rest):
                kind = z % 2 if gather else 1 - z % 2
                to_x = partner(x, kind) if step // 2 else x
                to_y = partner(y, kind) if step % 2 else y
                pairs.append(((x * along + y) * rest + z, (to_x * along + to_y) * rest + z))
    return lax.ppermute(block, ALL, pairs)


def on_device(valence, conduction, val_energy, cond_energy, frequencies, gvec_index, first_band):
    sent = density_call(valence, conduction, gvec_index)
    num_val = valence.shape[0]
    lines = 2 * num_val
    across = lax.axis_size("bx")
    along = lax.axis_size("by")
    group = lax.axis_size("grow") * lax.axis_size("zlo") * lax.axis_size("core")
    sent = sent.reshape(group, 2 * lines, 512)
    got = lax.all_to_all(sent, ZED, split_axis=0, concat_axis=0, tiled=True)
    cols = got[:, :lines].reshape(group * lines, 512)
    rows = got[:, lines:].reshape(group * lines, 512)
    x_here = lax.axis_index("bx")
    y_here = lax.axis_index("by")
    even = lax.axis_index("core") == 0

    def tile_of(place):
        return jnp.where(even, (place ^ (place >> 1)) & 1, place >> 1)

    def spot_of(place):
        return jnp.where(even, place >> 1, place & 1)

    tile = 2 * tile_of(x_here) + tile_of(y_here)
    spot = 2 * spot_of(x_here) + spot_of(y_here)
    blocks = {}
    for step in (0, 3, 2, 1):
        part = lax.dynamic_slice_in_dim(rows, (tile ^ step) * 128, 128, 1)
        block = jnp.concatenate([cols, part], 1)
        blocks[step] = exchange(block, step, True) if step else block
    steps = jnp.arange(4, dtype=jnp.int32)
    x_from = jnp.where(steps // 2 == 0, x_here, jnp.where(even, x_here ^ 1, 3 - x_here))
    y_from = jnp.where(steps % 2 == 0, y_here, jnp.where(even, y_here ^ 1, 3 - y_here))
    band = x_from * along + y_from
    bands = (band * group)[:, None] + jnp.arange(group, dtype=jnp.int32)
    energies = jnp.take(cond_energy, bands)
    gap = energies[..., None] - val_energy
    counted = bands[..., None] >= first_band
    ratio = -4.0 * gap[..., None] / (gap[..., None] ** 2 + frequencies**2)
    weight = jnp.where(counted[..., None], ratio, 0.0) / (cond_energy.shape[0] * num_val)
    weight = jnp.broadcast_to(weight[:, :, None], (across, group, 2, num_val, frequencies.shape[0]))
    weight = weight.reshape(across, group * lines, frequencies.shape[0])
    total, *pieces = product_call(spot.reshape(1), weight, [blocks[step] for step in range(4)])
    pieces = [exchange(pieces[step - 1], step, False) for step in (3, 2, 1)]
    return sum_call(total, pieces, (32, frequencies.shape[0], 2, 512))


def solution(mesh):
    fine = Mesh(mesh.devices.reshape(4, 4, 4, 2, 2), ALL)
    return jax.shard_map(
        on_device,
        mesh=fine,
        in_specs=(P(), P(ALL, None), P(), P(), P(), P(), P()),
        out_specs=P(("grow", "bx", "by"), None, None, ("zlo", "core")),
        check_vma=False,
    )
```

```python
import numpy as np
import jax
import jax.numpy as jnp
from jax import lax
from jax.experimental import pallas as pl
from jax.experimental.pallas import tpu as pltpu
from jax.sharding import Mesh, PartitionSpec as P
import ml_dtypes

GRID = 48
HALF = GRID // 2 + 1
BF = jnp.bfloat16
ZED = ("grow", "zlo", "core")
ALL = ("bx", "by") + ZED
CHUNKS = 4


def split_table(table):
    high = table.astype(ml_dtypes.bfloat16)
    low = (table - high.astype(np.float64)).astype(ml_dtypes.bfloat16)
    return high, low


def wave(left, right):
    angle = 2.0 * np.pi * (np.outer(left, right) % GRID) / GRID
    return np.cos(angle), np.sin(angle)


def tables():
    line = np.arange(GRID)
    cos, sin = wave(np.arange(HALF), line)
    first = np.zeros((2, HALF, 2, 4, 256))
    for odd in range(2):
        for b in range(4):
            at = 64 * odd + GRID * b
            first[odd, :, 0, b, at : at + GRID] = cos
            first[odd, :, 1, b, at : at + GRID] = -sin
    first = first.reshape(2, HALF * 8, 256)
    cos, sin = wave(line, line)
    order = np.zeros((2, GRID, 12, 2, 4))
    byb = cos.reshape(GRID, 12, 4)
    bys = sin.reshape(GRID, 12, 4)
    order[0, :, :, 0], order[0, :, :, 1] = byb, bys
    order[1, :, :, 0], order[1, :, :, 1] = -bys, byb
    second = order.reshape(2 * GRID, 2 * GRID)
    third = np.zeros((2, 2, GRID, 2, 128))
    for v in range(2):
        at = slice(GRID * v, GRID * v + GRID)
        third[v, 0, :, 0, at], third[v, 0, :, 1, at] = cos, sin
        third[v, 1, :, 0, at], third[v, 1, :, 1, at] = -sin, cos
    third = third.reshape(4 * GRID, 256)
    fh, fl = split_table(first)
    first = np.concatenate([fh, fl], 1)
    sh, sl = split_table(second)
    second = np.concatenate(
        [np.concatenate([sh, sh], 1), np.concatenate([sl, np.zeros_like(sl)], 1)], 0
    )
    th, tl = split_table(third)
    third = np.concatenate([th, tl], 0)
    return first, second, third


def dot_nt(a, b):
    return lax.dot_general(a, b, (((1,), (1,)), ((), ())), preferred_element_type=jnp.float32)


def dot_nn(a, b):
    return jnp.dot(a, b, preferred_element_type=jnp.float32)


def split(value):
    high = value.astype(BF)
    return high, (value - high.astype(jnp.float32)).astype(BF)


def density_kernel(
    cond_far, val_far, gvec_far, first_far, second_far, third_far, out,
    cond, val, gvec, prod, first, second, third, xh, xl, u, yh, yl, z, dens, sems,
):
    wide = xh.shape[1]
    chunk = GRID // CHUNKS
    loads = []
    for n in range(CHUNKS):
        lanes = pl.ds(wide * chunk * n, wide * chunk)
        loads.append(
            [
                pltpu.make_async_copy(far.at[:, lanes], near.at[:, lanes], sems.at[4 + 2 * n + m])
                for m, (far, near) in enumerate(((cond_far, cond), (val_far, val)))
            ]
        )
    far_near = ((first_far, first), (second_far, second), (third_far, third), (gvec_far, gvec))
    copies = [pltpu.make_async_copy(far, near, sems.at[n]) for n, (far, near) in enumerate(far_near)]
    for copy in sum(loads, []) + copies:
        copy.start()
    zero = jnp.zeros((32, xh.shape[1]), BF)
    for a in range(GRID):
        if a % chunk == 0:
            for load in loads[a // chunk]:
                load.wait()
        line = slice(wide * a, wide * a + wide)
        line = cond[:, line].astype(jnp.float32) * val[:, line].astype(jnp.float32)
        for tile in range(wide // 128):
            prod[tile, 4 * a : 4 * a + 4, :] = line[:, 128 * tile : 128 * tile + 128]
    for v in range(4):
        at = 128 * (v // 2) + GRID * (v % 2)
        for tile in range(wide // 128):
            high, low = split(prod[tile, pl.ds(v, GRID, stride=4), :])
            xh[at : at + GRID, 128 * tile : 128 * tile + 128] = high
            xl[at : at + GRID, 128 * tile : 128 * tile + 128] = low
    for p in range(2):
        xh[128 * p + 96 : 128 * p + 128, :] = zero
        xl[128 * p + 96 : 128 * p + 128, :] = zero
    n1 = HALF * 8
    for copy in copies:
        copy.wait()
    for pair in range(6):
        both = []
        for odd in range(2):
            start = 384 * pair + 128 * odd
            one = dot_nt(first[odd], xh[:, start : start + 256])
            two = dot_nt(first[odd, :n1], xl[:, start : start + 256])
            both.append((one[:n1] + one[n1:] + two).reshape(HALF, 8, 256))
        high, low = split(jnp.concatenate(both, 1))
        u[:, 16 * pair : 16 * pair + 16, :] = high
        u[:, 96 + 16 * pair : 96 + 16 * pair + 16, :] = low
    for start in range(0, HALF, 5):
        ks = range(start, start + 5)
        fulls = [dot_nn(second[...], u[k]) for k in ks]
        for k, full in zip(ks, fulls):
            high, low = split(full[:96] + full[96:])
            for p in range(2):
                for s in range(2):
                    rows, lanes = slice(GRID * s, GRID * s + GRID), slice(128 * p, 128 * p + 128)
                    put = (p, slice(GRID * k, GRID * k + GRID), slice(128 * s, 128 * s + 128))
                    yh[put] = high[rows, lanes]
                    yl[put] = low[rows, lanes]
    fill = yh.shape[1] - GRID * HALF
    blank = jnp.zeros((fill, 256), BF)
    for p in range(2):
        yh[p, GRID * HALF :, :] = blank
        yl[p, GRID * HALF :, :] = blank
        one = dot_nt(third[...], yh[p])
        two = dot_nt(third[:192], yl[p])
        z[192 * p : 192 * p + 192, :] = ((one[:192] + one[192:] + two) * GRID ** (-1.5)).astype(BF)
    for c in range(8):
        lanes = slice(256 * c, 256 * c + 256)
        g = gvec[:, lanes]
        plane = lax.shift_right_logical(lax.shift_right_logical(g, 4) * 43691, 17)
        k3 = g - plane * GRID
        k1 = lax.shift_right_logical(lax.shift_right_logical(plane, 4) * 43691, 17)
        k2 = plane - k1 * GRID
        flip = k3 >= HALF
        k1 = jnp.where(flip & (k1 > 0), GRID - k1, k1)
        k2 = jnp.where(flip & (k2 > 0), GRID - k2, k2)
        k3 = jnp.where(flip, GRID - k3, k3)
        spot = k3 * GRID + k2
        row = lax.broadcasted_iota(jnp.int32, (z.shape[1], 256), 0)
        hot = jnp.where(row == spot, 1.0, 0.0).astype(BF)
        t = dot_nn(z[...], hot)
        mask = lax.broadcasted_iota(jnp.int32, (GRID, 256), 0) == k1
        sign = jnp.where(flip, -1.0, 1.0)
        lines = []
        for s in range(2):
            for v in range(4):
                at = (2 * v + s) * GRID
                line = jnp.sum(jnp.where(mask, t[at : at + GRID], 0.0), 0, keepdims=True)
                lines.append(line * sign if s else line)
        dens[:, lanes] = jnp.concatenate(lines, 0)
    quarter = lax.broadcasted_iota(jnp.int32, (8, 128), 1) // 32
    for i in range(4):
        tiles = [dens[:, 512 * i + 128 * t : 512 * i + 128 * t + 128] for t in range(4)]
        turned = []
        for t in range(4):
            tile = tiles[t]
            for other in range(4):
                if other != t:
                    moved = pltpu.roll(tiles[other], (32 * (other - t)) % 128, 1)
                    tile = jnp.where(quarter == other, moved, tile)
            turned.append(tile)
        orders = (jnp.concatenate(tiles, 1), jnp.concatenate(turned, 1))
        for j in range(4):
            at = 16 * (4 * i + 2 * (j % 2) + j // 2)
            both = jnp.concatenate([dens[:, 512 * j : 512 * j + 512], orders[j % 2]], 0)
            out[at : at + 16, :] = both.astype(BF)


def density_call(valence, conduction, gvec_index):
    first, second, third = (jnp.asarray(t) for t in tables())
    gvec = gvec_index.reshape(1, -1)
    return pl.pallas_call(
        density_kernel,
        out_shape=jax.ShapeDtypeStruct((256, 512), BF),
        in_specs=[pl.BlockSpec(memory_space=pl.ANY)] * 6,
        out_specs=pl.BlockSpec(memory_space=pltpu.VMEM),
        scratch_shapes=[
            pltpu.VMEM(conduction.shape, BF),
            pltpu.VMEM(valence.shape, BF),
            pltpu.VMEM(gvec.shape, jnp.int32),
            pltpu.VMEM((GRID * GRID // 128, 4 * GRID, 128), jnp.float32),
            pltpu.VMEM(first.shape, BF),
            pltpu.VMEM(second.shape, BF),
            pltpu.VMEM(third.shape, BF),
            pltpu.VMEM((256, 2304), BF),
            pltpu.VMEM((256, 2304), BF),
            pltpu.VMEM((HALF, 192, 256), BF),
            pltpu.VMEM((2, 1280, 256), BF),
            pltpu.VMEM((2, 1280, 256), BF),
            pltpu.VMEM((384, 1280), BF),
            pltpu.VMEM((8, 2048), jnp.float32),
            pltpu.SemaphoreType.DMA((4 + 2 * CHUNKS,)),
        ],
        compiler_params=pltpu.CompilerParams(vmem_limit_bytes=60 * 1024 * 1024),
        cost_estimate=pl.CostEstimate(flops=5 * 10**9, bytes_accessed=3 * 10**6, transcendentals=0),
        name="density",
    )(conduction, valence, gvec, first, second, third)


def product_kernel(turn, weight, own, one, two, three, mine, first, second, third):
    blocks = (own, one, two, three)
    twice = []
    for block in blocks:
        rows = block[:, 512:640]
        parts = rows.astype(jnp.float32).reshape(16, 2, 4, 128)
        swapped = jnp.concatenate([parts[:, 1:], -parts[:, :1]], 1).reshape(128, 128)
        twice.append(jnp.concatenate([rows, swapped.astype(BF)], 1))
    lane = lax.broadcasted_iota(jnp.int32, (256, 512), 1)
    spot = ((lane // 128 + turn[0]) % 4) * 32 + (lane // 4) % 32 + 128 * (lane % 2)
    copies = jnp.where(lax.broadcasted_iota(jnp.int32, (256, 512), 0) == spot, 1.0, 0.0).astype(BF)
    spread = dot_nn(jnp.concatenate(twice, 0), copies)
    scale = weight[...].reshape(512, 2)
    early = (lax.broadcasted_iota(jnp.int32, (512, 512), 1) // 2) % 2 == 0
    left = (jnp.where(early, scale[:, 0:1], scale[:, 1:2]) * spread).astype(BF)
    right = jnp.concatenate([block[:, :512] for block in blocks], 0)
    total = lax.dot_general(left, right, (((0,), (0,)), ((), ())), preferred_element_type=jnp.float32)
    mine[...] = total[:128]
    first[...] = total[128:256].astype(BF)
    second[...] = total[256:384].astype(BF)
    third[...] = total[384:].astype(BF)


def product_call(turn, weight, blocks):
    piece = jax.ShapeDtypeStruct((128, 512), BF)
    vmem = pl.BlockSpec(memory_space=pltpu.VMEM)
    return pl.pallas_call(
        product_kernel,
        out_shape=(jax.ShapeDtypeStruct((128, 512), jnp.float32), piece, piece, piece),
        in_specs=[pl.BlockSpec(memory_space=pltpu.SMEM)] + [vmem] * 5,
        out_specs=(vmem,) * 4,
        compiler_params=pltpu.CompilerParams(vmem_limit_bytes=48 * 1024 * 1024),
        cost_estimate=pl.CostEstimate(flops=3 * 10**8, bytes_accessed=2 * 10**6, transcendentals=0),
        name="product",
    )(turn, weight, *blocks)


def ring_pairs(across, along, rest, step, gather):
    pairs = []
    for x in range(across):
        for y in range(along):
            for z in range(rest):
                if (z % 2 == 0) == gather:
                    to = ((x + step) % across, y)
                else:
                    to = (x, (y + step) % along)
                pairs.append(((x * along + y) * rest + z, (to[0] * along + to[1]) * rest + z))
    return pairs


def on_device(valence, conduction, val_energy, cond_energy, frequencies, gvec_index, first_band):
    sent = density_call(valence, conduction, gvec_index)
    num_val = valence.shape[0]
    lines = 2 * num_val
    across = lax.axis_size("bx")
    along = lax.axis_size("by")
    group = lax.axis_size("grow") * lax.axis_size("zlo") * lax.axis_size("core")
    sent = sent.reshape(group, 2 * lines, 512)
    got = lax.all_to_all(sent, ("grow", "core", "zlo"), split_axis=0, concat_axis=0, tiled=True)
    cols = got[:, :lines].reshape(group * lines, 512)
    rows = got[:, lines:].reshape(group * lines, 512)
    x_here = lax.axis_index("bx")
    y_here = lax.axis_index("by")
    even = lax.axis_index("core") == 0
    place = jnp.where(even, x_here, y_here)
    other = jnp.where(even, y_here, x_here)
    blocks = {}
    for step in (0, 1, 3, 2):
        target = lax.rem(place + step, across)
        part = lax.dynamic_slice_in_dim(rows, target * 128, 128, 1)
        block = jnp.concatenate([cols, part], 1)
        pairs = ring_pairs(across, along, group, step, True)
        blocks[step] = lax.ppermute(block, ALL, pairs) if step else block
    source = lax.rem(place - jnp.arange(across, dtype=jnp.int32) + across, across)
    band = jnp.where(even, source * along + other, other * along + source)
    chunk = jnp.arange(group, dtype=jnp.int32)
    bands = (band * group)[:, None] + chunk // 4 * 4 + chunk % 2 * 2 + chunk % 4 // 2
    energies = jnp.take(cond_energy, bands)
    gap = energies[..., None] - val_energy
    counted = bands[..., None] >= first_band
    ratio = -4.0 * gap[..., None] / (gap[..., None] ** 2 + frequencies**2)
    weight = jnp.where(counted[..., None], ratio, 0.0) / (cond_energy.shape[0] * num_val)
    weight = jnp.broadcast_to(weight[:, :, None], (across, group, 2, num_val, frequencies.shape[0]))
    weight = weight.reshape(across, group * lines, frequencies.shape[0])
    total, *pieces = product_call(other.reshape(1), weight, [blocks[step] for step in range(across)])
    for step in (1, 3, 2):
        pairs = ring_pairs(across, along, group, step, False)
        total = total + lax.ppermute(pieces[step - 1], ALL, pairs).astype(jnp.float32)
    return total.astype(BF).reshape(32, 2, 2, 512)


def solution(mesh):
    fine = Mesh(mesh.devices.reshape(4, 4, 4, 2, 2), ALL)
    return jax.shard_map(
        on_device,
        mesh=fine,
        in_specs=(P(), P(ALL, None), P(), P(), P(), P(), P()),
        out_specs=P(("grow", "bx", "by"), None, None, ("zlo", "core")),
        check_vma=False,
    )
```

```python
import numpy as np
import jax
import jax.numpy as jnp
from jax import lax
from jax.experimental import pallas as pl
from jax.experimental.pallas import tpu as pltpu
from jax.sharding import Mesh, PartitionSpec as P
import ml_dtypes

GRID = 48
HALF = GRID // 2 + 1
BF = jnp.bfloat16
ZED = ("grow", "zlo", "core")
ALL = ("bx", "by") + ZED
CHUNKS = 4


def split_table(table):
    high = table.astype(ml_dtypes.bfloat16)
    low = (table - high.astype(np.float64)).astype(ml_dtypes.bfloat16)
    return high, low


def wave(left, right):
    angle = 2.0 * np.pi * (np.outer(left, right) % GRID) / GRID
    return np.cos(angle), np.sin(angle)


def tables():
    line = np.arange(GRID)
    cos, sin = wave(np.arange(HALF), line)
    first = np.zeros((2, HALF, 2, 4, 256))
    for odd in range(2):
        for b in range(4):
            at = 64 * odd + GRID * b
            first[odd, :, 0, b, at : at + GRID] = cos
            first[odd, :, 1, b, at : at + GRID] = -sin
    first = first.reshape(2, HALF * 8, 256)
    cos, sin = wave(line, line)
    order = np.zeros((2, GRID, 12, 2, 4))
    byb = cos.reshape(GRID, 12, 4)
    bys = sin.reshape(GRID, 12, 4)
    order[0, :, :, 0], order[0, :, :, 1] = byb, bys
    order[1, :, :, 0], order[1, :, :, 1] = -bys, byb
    second = order.reshape(2 * GRID, 2 * GRID)
    third = np.zeros((2, 2, GRID, 2, 128))
    for v in range(2):
        at = slice(GRID * v, GRID * v + GRID)
        third[v, 0, :, 0, at], third[v, 0, :, 1, at] = cos, sin
        third[v, 1, :, 0, at], third[v, 1, :, 1, at] = -sin, cos
    third = third.reshape(4 * GRID, 256)
    fh, fl = split_table(first)
    first = np.concatenate([fh, fl], 1)
    sh, sl = split_table(second)
    second = np.concatenate(
        [np.concatenate([sh, sh], 1), np.concatenate([sl, np.zeros_like(sl)], 1)], 0
    )
    th, tl = split_table(third)
    third = np.concatenate([th, tl], 0)
    return first, second, third


def dot_nt(a, b):
    return lax.dot_general(a, b, (((1,), (1,)), ((), ())), preferred_element_type=jnp.float32)


def dot_nn(a, b):
    return jnp.dot(a, b, preferred_element_type=jnp.float32)


def split(value):
    high = value.astype(BF)
    return high, (value - high.astype(jnp.float32)).astype(BF)


MEMBERS = (((0, 1), (2, 3)), ((0, 3), (1, 2)))


def reduce_order(tiles, quarter, kind):
    result = []
    for xs in MEMBERS[kind]:
        for ys in MEMBERS[kind]:
            made = None
            for n in range(4):
                x, y = xs[n // 2], ys[n % 2]
                shift = 32 * (n - y) % 128
                moved = pltpu.roll(tiles[x], shift, 1) if shift else tiles[x]
                made = moved if made is None else jnp.where(quarter == n, moved, made)
            result.append(made)
    return jnp.concatenate(result, 1)


def density_kernel(
    cond_far, val_far, gvec_far, first_far, second_far, third_far, out,
    cond, val, gvec, prod, first, second, third, xh, xl, u, yh, yl, z, dens, sems,
):
    wide = xh.shape[1]
    chunk = GRID // CHUNKS
    loads = []
    for n in range(CHUNKS):
        lanes = pl.ds(wide * chunk * n, wide * chunk)
        loads.append(
            [
                pltpu.make_async_copy(far.at[:, lanes], near.at[:, lanes], sems.at[4 + 2 * n + m])
                for m, (far, near) in enumerate(((cond_far, cond), (val_far, val)))
            ]
        )
    far_near = ((first_far, first), (second_far, second), (third_far, third), (gvec_far, gvec))
    copies = [pltpu.make_async_copy(far, near, sems.at[n]) for n, (far, near) in enumerate(far_near)]
    for copy in sum(loads, []) + copies:
        copy.start()
    zero = jnp.zeros((32, xh.shape[1]), BF)
    for a in range(GRID):
        if a % chunk == 0:
            for load in loads[a // chunk]:
                load.wait()
        line = slice(wide * a, wide * a + wide)
        line = cond[:, line].astype(jnp.float32) * val[:, line].astype(jnp.float32)
        for tile in range(wide // 128):
            prod[tile, 4 * a : 4 * a + 4, :] = line[:, 128 * tile : 128 * tile + 128]
    for v in range(4):
        at = 128 * (v // 2) + GRID * (v % 2)
        for tile in range(wide // 128):
            high, low = split(prod[tile, pl.ds(v, GRID, stride=4), :])
            xh[at : at + GRID, 128 * tile : 128 * tile + 128] = high
            xl[at : at + GRID, 128 * tile : 128 * tile + 128] = low
    for p in range(2):
        xh[128 * p + 96 : 128 * p + 128, :] = zero
        xl[128 * p + 96 : 128 * p + 128, :] = zero
    n1 = HALF * 8
    for copy in copies:
        copy.wait()
    for pair in range(6):
        both = []
        for odd in range(2):
            start = 384 * pair + 128 * odd
            one = dot_nt(first[odd], xh[:, start : start + 256])
            two = dot_nt(first[odd, :n1], xl[:, start : start + 256])
            both.append((one[:n1] + one[n1:] + two).reshape(HALF, 8, 256))
        high, low = split(jnp.concatenate(both, 1))
        u[:, 16 * pair : 16 * pair + 16, :] = high
        u[:, 96 + 16 * pair : 96 + 16 * pair + 16, :] = low
    for start in range(0, HALF, 5):
        ks = range(start, start + 5)
        fulls = [dot_nn(second[...], u[k]) for k in ks]
        for k, full in zip(ks, fulls):
            high, low = split(full[:96] + full[96:])
            for p in range(2):
                for s in range(2):
                    rows, lanes = slice(GRID * s, GRID * s + GRID), slice(128 * p, 128 * p + 128)
                    put = (p, slice(GRID * k, GRID * k + GRID), slice(128 * s, 128 * s + 128))
                    yh[put] = high[rows, lanes]
                    yl[put] = low[rows, lanes]
    fill = yh.shape[1] - GRID * HALF
    blank = jnp.zeros((fill, 256), BF)
    for p in range(2):
        yh[p, GRID * HALF :, :] = blank
        yl[p, GRID * HALF :, :] = blank
        one = dot_nt(third[...], yh[p])
        two = dot_nt(third[:192], yl[p])
        z[192 * p : 192 * p + 192, :] = ((one[:192] + one[192:] + two) * GRID ** (-1.5)).astype(BF)
    for c in range(8):
        lanes = slice(256 * c, 256 * c + 256)
        g = gvec[:, lanes]
        plane = lax.shift_right_logical(lax.shift_right_logical(g, 4) * 43691, 17)
        k3 = g - plane * GRID
        k1 = lax.shift_right_logical(lax.shift_right_logical(plane, 4) * 43691, 17)
        k2 = plane - k1 * GRID
        flip = k3 >= HALF
        k1 = jnp.where(flip & (k1 > 0), GRID - k1, k1)
        k2 = jnp.where(flip & (k2 > 0), GRID - k2, k2)
        k3 = jnp.where(flip, GRID - k3, k3)
        spot = k3 * GRID + k2
        row = lax.broadcasted_iota(jnp.int32, (z.shape[1], 256), 0)
        hot = jnp.where(row == spot, 1.0, 0.0).astype(BF)
        t = dot_nn(z[...], hot)
        mask = lax.broadcasted_iota(jnp.int32, (GRID, 256), 0) == k1
        sign = jnp.where(flip, -1.0, 1.0)
        lines = []
        for s in range(2):
            for v in range(4):
                at = (2 * v + s) * GRID
                line = jnp.sum(jnp.where(mask, t[at : at + GRID], 0.0), 0, keepdims=True)
                lines.append(line * sign if s else line)
        dens[:, lanes] = jnp.concatenate(lines, 0)
    quarter = lax.broadcasted_iota(jnp.int32, (8, 128), 1) // 32
    for i in range(4):
        tiles = [dens[:, 512 * i + 128 * t : 512 * i + 128 * t + 128] for t in range(4)]
        orders = [reduce_order(tiles, quarter, kind) for kind in (1, 0)]
        for j in range(4):
            at = 16 * (4 * i + 2 * (j % 2) + j // 2)
            both = jnp.concatenate([dens[:, 512 * j : 512 * j + 512], orders[j % 2]], 0)
            out[at : at + 16, :] = both.astype(BF)


def density_call(valence, conduction, gvec_index):
    first, second, third = (jnp.asarray(t) for t in tables())
    gvec = gvec_index.reshape(1, -1)
    return pl.pallas_call(
        density_kernel,
        out_shape=jax.ShapeDtypeStruct((256, 512), BF),
        in_specs=[pl.BlockSpec(memory_space=pl.ANY)] * 6,
        out_specs=pl.BlockSpec(memory_space=pltpu.VMEM),
        scratch_shapes=[
            pltpu.VMEM(conduction.shape, BF),
            pltpu.VMEM(valence.shape, BF),
            pltpu.VMEM(gvec.shape, jnp.int32),
            pltpu.VMEM((GRID * GRID // 128, 4 * GRID, 128), jnp.float32),
            pltpu.VMEM(first.shape, BF),
            pltpu.VMEM(second.shape, BF),
            pltpu.VMEM(third.shape, BF),
            pltpu.VMEM((256, 2304), BF),
            pltpu.VMEM((256, 2304), BF),
            pltpu.VMEM((HALF, 192, 256), BF),
            pltpu.VMEM((2, 1280, 256), BF),
            pltpu.VMEM((2, 1280, 256), BF),
            pltpu.VMEM((384, 1280), BF),
            pltpu.VMEM((8, 2048), jnp.float32),
            pltpu.SemaphoreType.DMA((4 + 2 * CHUNKS,)),
        ],
        compiler_params=pltpu.CompilerParams(vmem_limit_bytes=60 * 1024 * 1024),
        cost_estimate=pl.CostEstimate(flops=5 * 10**9, bytes_accessed=3 * 10**6, transcendentals=0),
        name="density",
    )(conduction, valence, gvec, first, second, third)


def product_kernel(turn, weight, own, one, two, three, mine, first, second, third):
    blocks = (own, one, two, three)
    twice = []
    for block in blocks:
        rows = block[:, 512:640]
        parts = rows.astype(jnp.float32).reshape(16, 2, 4, 128)
        swapped = jnp.concatenate([parts[:, 1:], -parts[:, :1]], 1).reshape(128, 128)
        twice.append(jnp.concatenate([rows, swapped.astype(BF)], 1))
    lane = lax.broadcasted_iota(jnp.int32, (256, 512), 1)
    spot = ((lane // 128) ^ turn[0]) * 32 + (lane // 4) % 32 + 128 * (lane % 2)
    copies = jnp.where(lax.broadcasted_iota(jnp.int32, (256, 512), 0) == spot, 1.0, 0.0).astype(BF)
    spread = dot_nn(jnp.concatenate(twice, 0), copies)
    scale = weight[...].reshape(512, 2)
    early = (lax.broadcasted_iota(jnp.int32, (512, 512), 1) // 2) % 2 == 0
    left = (jnp.where(early, scale[:, 0:1], scale[:, 1:2]) * spread).astype(BF)
    right = jnp.concatenate([block[:, :512] for block in blocks], 0)
    total = lax.dot_general(left, right, (((0,), (0,)), ((), ())), preferred_element_type=jnp.float32)
    mine[...] = total[:128]
    first[...] = total[128:256].astype(BF)
    second[...] = total[256:384].astype(BF)
    third[...] = total[384:].astype(BF)


def product_call(turn, weight, blocks):
    piece = jax.ShapeDtypeStruct((128, 512), BF)
    vmem = pl.BlockSpec(memory_space=pltpu.VMEM)
    return pl.pallas_call(
        product_kernel,
        out_shape=(jax.ShapeDtypeStruct((128, 512), jnp.float32), piece, piece, piece),
        in_specs=[pl.BlockSpec(memory_space=pltpu.SMEM)] + [vmem] * 5,
        out_specs=(vmem,) * 4,
        compiler_params=pltpu.CompilerParams(vmem_limit_bytes=48 * 1024 * 1024),
        cost_estimate=pl.CostEstimate(flops=3 * 10**8, bytes_accessed=2 * 10**6, transcendentals=0),
        name="product",
    )(turn, weight, *blocks)


def exchange(block, step, gather):
    across, along = lax.axis_size("bx"), lax.axis_size("by")
    rest = lax.axis_size("grow") * lax.axis_size("zlo") * lax.axis_size("core")

    def partner(place, kind):
        return 3 - place if kind else place ^ 1

    pairs = []
    for x in range(across):
        for y in range(along):
            for z in range(rest):
                kind = z % 2 if gather else 1 - z % 2
                to_x = partner(x, kind) if step // 2 else x
                to_y = partner(y, kind) if step % 2 else y
                pairs.append(((x * along + y) * rest + z, (to_x * along + to_y) * rest + z))
    return lax.ppermute(block, ALL, pairs)


def on_device(valence, conduction, val_energy, cond_energy, frequencies, gvec_index, first_band):
    sent = density_call(valence, conduction, gvec_index)
    num_val = valence.shape[0]
    lines = 2 * num_val
    across = lax.axis_size("bx")
    along = lax.axis_size("by")
    group = lax.axis_size("grow") * lax.axis_size("zlo") * lax.axis_size("core")
    sent = sent.reshape(group, 2 * lines, 512)
    got = lax.all_to_all(sent, ("grow", "core", "zlo"), split_axis=0, concat_axis=0, tiled=True)
    cols = got[:, :lines].reshape(group * lines, 512)
    rows = got[:, lines:].reshape(group * lines, 512)
    x_here = lax.axis_index("bx")
    y_here = lax.axis_index("by")
    even = lax.axis_index("core") == 0

    def tile_of(place):
        return jnp.where(even, (place ^ (place >> 1)) & 1, place >> 1)

    def spot_of(place):
        return jnp.where(even, place >> 1, place & 1)

    tile = 2 * tile_of(x_here) + tile_of(y_here)
    spot = 2 * spot_of(x_here) + spot_of(y_here)
    blocks = {}
    for step in (0, 3, 2, 1):
        part = lax.dynamic_slice_in_dim(rows, (tile ^ step) * 128, 128, 1)
        block = jnp.concatenate([cols, part], 1)
        blocks[step] = exchange(block, step, True) if step else block
    steps = jnp.arange(4, dtype=jnp.int32)
    x_from = jnp.where(steps // 2 == 0, x_here, jnp.where(even, x_here ^ 1, 3 - x_here))
    y_from = jnp.where(steps % 2 == 0, y_here, jnp.where(even, y_here ^ 1, 3 - y_here))
    band = x_from * along + y_from
    chunk = jnp.arange(group, dtype=jnp.int32)
    bands = (band * group)[:, None] + chunk // 4 * 4 + chunk % 2 * 2 + chunk % 4 // 2
    energies = jnp.take(cond_energy, bands)
    gap = energies[..., None] - val_energy
    counted = bands[..., None] >= first_band
    ratio = -4.0 * gap[..., None] / (gap[..., None] ** 2 + frequencies**2)
    weight = jnp.where(counted[..., None], ratio, 0.0) / (cond_energy.shape[0] * num_val)
    weight = jnp.broadcast_to(weight[:, :, None], (across, group, 2, num_val, frequencies.shape[0]))
    weight = weight.reshape(across, group * lines, frequencies.shape[0])
    total, *pieces = product_call(spot.reshape(1), weight, [blocks[step] for step in range(4)])
    for step in (3, 2, 1):
        total = total + exchange(pieces[step - 1], step, False).astype(jnp.float32)
    return total.astype(BF).reshape(32, frequencies.shape[0], 2, 512)


def solution(mesh):
    fine = Mesh(mesh.devices.reshape(4, 4, 4, 2, 2), ALL)
    return jax.shard_map(
        on_device,
        mesh=fine,
        in_specs=(P(), P(ALL, None), P(), P(), P(), P(), P()),
        out_specs=P(("grow", "bx", "by"), None, None, ("zlo", "core")),
        check_vma=False,
    )
```

```python
import numpy as np
import jax
import jax.numpy as jnp
from jax import lax
from jax.experimental import pallas as pl
from jax.experimental.pallas import tpu as pltpu
from jax.sharding import Mesh, PartitionSpec as P
import ml_dtypes

GRID = 48
HALF = GRID // 2 + 1
BF = jnp.bfloat16
ZED = ("grow", "zlo", "core")
ALL = ("bx", "by") + ZED
CHUNKS = 4


def split_table(table):
    high = table.astype(ml_dtypes.bfloat16)
    low = (table - high.astype(np.float64)).astype(ml_dtypes.bfloat16)
    return high, low


def wave(left, right):
    angle = 2.0 * np.pi * (np.outer(left, right) % GRID) / GRID
    return np.cos(angle), np.sin(angle)


def tables():
    line = np.arange(GRID)
    cos, sin = wave(np.arange(HALF), line)
    first = np.zeros((2, HALF, 2, 4, 256))
    for odd in range(2):
        for b in range(4):
            at = 64 * odd + GRID * b
            first[odd, :, 0, b, at : at + GRID] = cos
            first[odd, :, 1, b, at : at + GRID] = -sin
    first = first.reshape(2, HALF * 8, 256)
    cos, sin = wave(line, line)
    order = np.zeros((2, GRID, 12, 2, 4))
    byb = cos.reshape(GRID, 12, 4)
    bys = sin.reshape(GRID, 12, 4)
    order[0, :, :, 0], order[0, :, :, 1] = byb, bys
    order[1, :, :, 0], order[1, :, :, 1] = -bys, byb
    second = order.reshape(2 * GRID, 2 * GRID)
    third = np.zeros((2, 2, GRID, 2, 128))
    for v in range(2):
        at = slice(GRID * v, GRID * v + GRID)
        third[v, 0, :, 0, at], third[v, 0, :, 1, at] = cos, sin
        third[v, 1, :, 0, at], third[v, 1, :, 1, at] = -sin, cos
    third = third.reshape(4 * GRID, 256)
    fh, fl = split_table(first)
    first = np.concatenate([fh, fl], 1)
    sh, sl = split_table(second)
    second = np.concatenate(
        [np.concatenate([sh, sh], 1), np.concatenate([sl, np.zeros_like(sl)], 1)], 0
    )
    th, tl = split_table(third)
    third = np.concatenate([th, tl], 0)
    return first, second, third


def dot_nt(a, b):
    return lax.dot_general(a, b, (((1,), (1,)), ((), ())), preferred_element_type=jnp.float32)


def dot_nn(a, b):
    return jnp.dot(a, b, preferred_element_type=jnp.float32)


def split(value):
    high = value.astype(BF)
    return high, (value - high.astype(jnp.float32)).astype(BF)


MEMBERS = (((0, 1), (2, 3)), ((0, 3), (1, 2)))


def reduce_order(tiles, quarter, kind):
    result = []
    for xs in MEMBERS[kind]:
        for ys in MEMBERS[kind]:
            made = None
            for n in range(4):
                x, y = xs[n // 2], ys[n % 2]
                shift = 32 * (n - y) % 128
                moved = pltpu.roll(tiles[x], shift, 1) if shift else tiles[x]
                made = moved if made is None else jnp.where(quarter == n, moved, made)
            result.append(made)
    return jnp.concatenate(result, 1)


def density_kernel(
    cond_far, val_far, gvec_far, first_far, second_far, third_far, out,
    cond, val, gvec, prod, first, second, third, xh, xl, u, yh, yl, z, dens, sems,
):
    wide = xh.shape[1]
    chunk = GRID // CHUNKS
    loads = []
    for n in range(CHUNKS):
        lanes = pl.ds(wide * chunk * n, wide * chunk)
        loads.append(
            [
                pltpu.make_async_copy(far.at[:, lanes], near.at[:, lanes], sems.at[4 + 2 * n + m])
                for m, (far, near) in enumerate(((cond_far, cond), (val_far, val)))
            ]
        )
    far_near = ((first_far, first), (second_far, second), (third_far, third), (gvec_far, gvec))
    copies = [pltpu.make_async_copy(far, near, sems.at[n]) for n, (far, near) in enumerate(far_near)]
    for copy in sum(loads, []) + copies:
        copy.start()
    zero = jnp.zeros((32, xh.shape[1]), BF)
    for a in range(GRID):
        if a % chunk == 0:
            for load in loads[a // chunk]:
                load.wait()
        line = slice(wide * a, wide * a + wide)
        line = cond[:, line].astype(jnp.float32) * val[:, line].astype(jnp.float32)
        for tile in range(wide // 128):
            prod[tile, 4 * a : 4 * a + 4, :] = line[:, 128 * tile : 128 * tile + 128]
    for v in range(4):
        at = 128 * (v // 2) + GRID * (v % 2)
        for tile in range(wide // 128):
            high, low = split(prod[tile, pl.ds(v, GRID, stride=4), :])
            xh[at : at + GRID, 128 * tile : 128 * tile + 128] = high
            xl[at : at + GRID, 128 * tile : 128 * tile + 128] = low
    for p in range(2):
        xh[128 * p + 96 : 128 * p + 128, :] = zero
        xl[128 * p + 96 : 128 * p + 128, :] = zero
    n1 = HALF * 8
    for copy in copies:
        copy.wait()
    for pair in range(6):
        both = []
        for odd in range(2):
            start = 384 * pair + 128 * odd
            one = dot_nt(first[odd], xh[:, start : start + 256])
            two = dot_nt(first[odd, :n1], xl[:, start : start + 256])
            both.append((one[:n1] + one[n1:] + two).reshape(HALF, 8, 256))
        high, low = split(jnp.concatenate(both, 1))
        u[:, 16 * pair : 16 * pair + 16, :] = high
        u[:, 96 + 16 * pair : 96 + 16 * pair + 16, :] = low
    for start in range(0, HALF, 5):
        ks = range(start, start + 5)
        fulls = [dot_nn(second[...], u[k]) for k in ks]
        for k, full in zip(ks, fulls):
            high, low = split(full[:96] + full[96:])
            for p in range(2):
                for s in range(2):
                    rows, lanes = slice(GRID * s, GRID * s + GRID), slice(128 * p, 128 * p + 128)
                    put = (p, slice(GRID * k, GRID * k + GRID), slice(128 * s, 128 * s + 128))
                    yh[put] = high[rows, lanes]
                    yl[put] = low[rows, lanes]
    fill = yh.shape[1] - GRID * HALF
    blank = jnp.zeros((fill, 256), BF)
    for p in range(2):
        yh[p, GRID * HALF :, :] = blank
        yl[p, GRID * HALF :, :] = blank
        one = dot_nt(third[...], yh[p])
        two = dot_nt(third[:192], yl[p])
        z[192 * p : 192 * p + 192, :] = ((one[:192] + one[192:] + two) * GRID ** (-1.5)).astype(BF)
    for c in range(8):
        lanes = slice(256 * c, 256 * c + 256)
        g = gvec[:, lanes]
        plane = lax.shift_right_logical(lax.shift_right_logical(g, 4) * 43691, 17)
        k3 = g - plane * GRID
        k1 = lax.shift_right_logical(lax.shift_right_logical(plane, 4) * 43691, 17)
        k2 = plane - k1 * GRID
        flip = k3 >= HALF
        k1 = jnp.where(flip & (k1 > 0), GRID - k1, k1)
        k2 = jnp.where(flip & (k2 > 0), GRID - k2, k2)
        k3 = jnp.where(flip, GRID - k3, k3)
        spot = k3 * GRID + k2
        row = lax.broadcasted_iota(jnp.int32, (z.shape[1], 256), 0)
        hot = jnp.where(row == spot, 1.0, 0.0).astype(BF)
        t = dot_nn(z[...], hot)
        mask = lax.broadcasted_iota(jnp.int32, (GRID, 256), 0) == k1
        sign = jnp.where(flip, -1.0, 1.0)
        lines = []
        for s in range(2):
            for v in range(4):
                at = (2 * v + s) * GRID
                line = jnp.sum(jnp.where(mask, t[at : at + GRID], 0.0), 0, keepdims=True)
                lines.append(line * sign if s else line)
        dens[:, lanes] = jnp.concatenate(lines, 0)
    quarter = lax.broadcasted_iota(jnp.int32, (8, 128), 1) // 32
    for i in range(4):
        tiles = [dens[:, 512 * i + 128 * t : 512 * i + 128 * t + 128] for t in range(4)]
        orders = [reduce_order(tiles, quarter, kind) for kind in (0, 1)]
        for j in range(4):
            at = 16 * (4 * i + 2 * (j % 2) + j // 2)
            both = jnp.concatenate([dens[:, 512 * j : 512 * j + 512], orders[j % 2]], 0)
            out[at : at + 16, :] = both.astype(BF)


def density_call(valence, conduction, gvec_index):
    first, second, third = (jnp.asarray(t) for t in tables())
    gvec = gvec_index.reshape(1, -1)
    return pl.pallas_call(
        density_kernel,
        out_shape=jax.ShapeDtypeStruct((256, 512), BF),
        in_specs=[pl.BlockSpec(memory_space=pl.ANY)] * 6,
        out_specs=pl.BlockSpec(memory_space=pltpu.VMEM),
        scratch_shapes=[
            pltpu.VMEM(conduction.shape, BF),
            pltpu.VMEM(valence.shape, BF),
            pltpu.VMEM(gvec.shape, jnp.int32),
            pltpu.VMEM((GRID * GRID // 128, 4 * GRID, 128), jnp.float32),
            pltpu.VMEM(first.shape, BF),
            pltpu.VMEM(second.shape, BF),
            pltpu.VMEM(third.shape, BF),
            pltpu.VMEM((256, 2304), BF),
            pltpu.VMEM((256, 2304), BF),
            pltpu.VMEM((HALF, 192, 256), BF),
            pltpu.VMEM((2, 1280, 256), BF),
            pltpu.VMEM((2, 1280, 256), BF),
            pltpu.VMEM((384, 1280), BF),
            pltpu.VMEM((8, 2048), jnp.float32),
            pltpu.SemaphoreType.DMA((4 + 2 * CHUNKS,)),
        ],
        compiler_params=pltpu.CompilerParams(vmem_limit_bytes=60 * 1024 * 1024),
        cost_estimate=pl.CostEstimate(flops=5 * 10**9, bytes_accessed=3 * 10**6, transcendentals=0),
        name="density",
    )(conduction, valence, gvec, first, second, third)


def product_kernel(turn, weight, own, one, two, three, mine, first, second, third):
    blocks = (own, one, two, three)
    twice = []
    for block in blocks:
        rows = block[:, 512:640]
        parts = rows.astype(jnp.float32).reshape(16, 2, 4, 128)
        swapped = jnp.concatenate([parts[:, 1:], -parts[:, :1]], 1).reshape(128, 128)
        twice.append(jnp.concatenate([rows, swapped.astype(BF)], 1))
    lane = lax.broadcasted_iota(jnp.int32, (256, 512), 1)
    spot = ((lane // 128) ^ turn[0]) * 32 + (lane // 4) % 32 + 128 * (lane % 2)
    copies = jnp.where(lax.broadcasted_iota(jnp.int32, (256, 512), 0) == spot, 1.0, 0.0).astype(BF)
    spread = dot_nn(jnp.concatenate(twice, 0), copies)
    scale = weight[...].reshape(512, 2)
    early = (lax.broadcasted_iota(jnp.int32, (512, 512), 1) // 2) % 2 == 0
    left = (jnp.where(early, scale[:, 0:1], scale[:, 1:2]) * spread).astype(BF)
    right = jnp.concatenate([block[:, :512] for block in blocks], 0)
    total = lax.dot_general(left, right, (((0,), (0,)), ((), ())), preferred_element_type=jnp.float32)
    mine[...] = total[:128]
    first[...] = total[128:256].astype(BF)
    second[...] = total[256:384].astype(BF)
    third[...] = total[384:].astype(BF)


def product_call(turn, weight, blocks):
    piece = jax.ShapeDtypeStruct((128, 512), BF)
    vmem = pl.BlockSpec(memory_space=pltpu.VMEM)
    return pl.pallas_call(
        product_kernel,
        out_shape=(jax.ShapeDtypeStruct((128, 512), jnp.float32), piece, piece, piece),
        in_specs=[pl.BlockSpec(memory_space=pltpu.SMEM)] + [vmem] * 5,
        out_specs=(vmem,) * 4,
        compiler_params=pltpu.CompilerParams(vmem_limit_bytes=48 * 1024 * 1024),
        cost_estimate=pl.CostEstimate(flops=3 * 10**8, bytes_accessed=2 * 10**6, transcendentals=0),
        name="product",
    )(turn, weight, *blocks)


def exchange(block, step, gather):
    across, along = lax.axis_size("bx"), lax.axis_size("by")
    rest = lax.axis_size("grow") * lax.axis_size("zlo") * lax.axis_size("core")

    def partner(place, kind):
        return 3 - place if kind else place ^ 1

    pairs = []
    for x in range(across):
        for y in range(along):
            for z in range(rest):
                kind = 1 - z % 2 if gather else z % 2
                to_x = partner(x, kind) if step // 2 else x
                to_y = partner(y, kind) if step % 2 else y
                pairs.append(((x * along + y) * rest + z, (to_x * along + to_y) * rest + z))
    return lax.ppermute(block, ALL, pairs)


def on_device(valence, conduction, val_energy, cond_energy, frequencies, gvec_index, first_band):
    sent = density_call(valence, conduction, gvec_index)
    num_val = valence.shape[0]
    lines = 2 * num_val
    across = lax.axis_size("bx")
    along = lax.axis_size("by")
    group = lax.axis_size("grow") * lax.axis_size("zlo") * lax.axis_size("core")
    sent = sent.reshape(group, 2 * lines, 512)
    got = lax.all_to_all(sent, ("grow", "core", "zlo"), split_axis=0, concat_axis=0, tiled=True)
    cols = got[:, :lines].reshape(group * lines, 512)
    rows = got[:, lines:].reshape(group * lines, 512)
    x_here = lax.axis_index("bx")
    y_here = lax.axis_index("by")
    even = lax.axis_index("core") == 1

    def tile_of(place):
        return jnp.where(even, (place ^ (place >> 1)) & 1, place >> 1)

    def spot_of(place):
        return jnp.where(even, place >> 1, place & 1)

    tile = 2 * tile_of(x_here) + tile_of(y_here)
    spot = 2 * spot_of(x_here) + spot_of(y_here)
    blocks = {}
    for step in (0, 3, 2, 1):
        part = lax.dynamic_slice_in_dim(rows, (tile ^ step) * 128, 128, 1)
        block = jnp.concatenate([cols, part], 1)
        blocks[step] = exchange(block, step, True) if step else block
    steps = jnp.arange(4, dtype=jnp.int32)
    x_from = jnp.where(steps // 2 == 0, x_here, jnp.where(even, x_here ^ 1, 3 - x_here))
    y_from = jnp.where(steps % 2 == 0, y_here, jnp.where(even, y_here ^ 1, 3 - y_here))
    band = x_from * along + y_from
    chunk = jnp.arange(group, dtype=jnp.int32)
    bands = (band * group)[:, None] + chunk // 4 * 4 + chunk % 2 * 2 + chunk % 4 // 2
    energies = jnp.take(cond_energy, bands)
    gap = energies[..., None] - val_energy
    counted = bands[..., None] >= first_band
    ratio = -4.0 * gap[..., None] / (gap[..., None] ** 2 + frequencies**2)
    weight = jnp.where(counted[..., None], ratio, 0.0) / (cond_energy.shape[0] * num_val)
    weight = jnp.broadcast_to(weight[:, :, None], (across, group, 2, num_val, frequencies.shape[0]))
    weight = weight.reshape(across, group * lines, frequencies.shape[0])
    total, *pieces = product_call(spot.reshape(1), weight, [blocks[step] for step in range(4)])
    for step in (3, 2, 1):
        total = total + exchange(pieces[step - 1], step, False).astype(jnp.float32)
    return total.astype(BF).reshape(32, frequencies.shape[0], 2, 512)


def solution(mesh):
    fine = Mesh(mesh.devices.reshape(4, 4, 4, 2, 2), ALL)
    return jax.shard_map(
        on_device,
        mesh=fine,
        in_specs=(P(), P(ALL, None), P(), P(), P(), P(), P()),
        out_specs=P(("grow", "bx", "by"), None, None, ("zlo", "core")),
        check_vma=False,
    )
```

```python
import numpy as np
import jax
import jax.numpy as jnp
from jax import lax
from jax.experimental import pallas as pl
from jax.experimental.pallas import tpu as pltpu
from jax.sharding import Mesh, PartitionSpec as P
import ml_dtypes

GRID = 48
HALF = GRID // 2 + 1
BF = jnp.bfloat16
ZED = ("grow", "zlo", "core")
ALL = ("bx", "by") + ZED
CHUNKS = 4


def split_table(table):
    high = table.astype(ml_dtypes.bfloat16)
    low = (table - high.astype(np.float64)).astype(ml_dtypes.bfloat16)
    return high, low


def wave(left, right):
    angle = 2.0 * np.pi * (np.outer(left, right) % GRID) / GRID
    return np.cos(angle), np.sin(angle)


def tables():
    line = np.arange(GRID)
    cos, sin = wave(np.arange(HALF), line)
    first = np.zeros((2, HALF, 2, 4, 256))
    for odd in range(2):
        for b in range(4):
            at = 64 * odd + GRID * b
            first[odd, :, 0, b, at : at + GRID] = cos
            first[odd, :, 1, b, at : at + GRID] = -sin
    first = first.reshape(2, HALF * 8, 256)
    cos, sin = wave(line, line)
    order = np.zeros((2, GRID, 12, 2, 4))
    byb = cos.reshape(GRID, 12, 4)
    bys = sin.reshape(GRID, 12, 4)
    order[0, :, :, 0], order[0, :, :, 1] = byb, bys
    order[1, :, :, 0], order[1, :, :, 1] = -bys, byb
    second = order.reshape(2 * GRID, 2 * GRID)
    third = np.zeros((2, 2, GRID, 2, 128))
    for v in range(2):
        at = slice(GRID * v, GRID * v + GRID)
        third[v, 0, :, 0, at], third[v, 0, :, 1, at] = cos, sin
        third[v, 1, :, 0, at], third[v, 1, :, 1, at] = -sin, cos
    third = third.reshape(4 * GRID, 256)
    fh, fl = split_table(first)
    first = np.concatenate([fh, fl], 1)
    sh, sl = split_table(second)
    second = np.concatenate(
        [np.concatenate([sh, sh], 1), np.concatenate([sl, np.zeros_like(sl)], 1)], 0
    )
    th, tl = split_table(third)
    third = np.concatenate([th, tl], 0)
    return first, second, third


def dot_nt(a, b):
    return lax.dot_general(a, b, (((1,), (1,)), ((), ())), preferred_element_type=jnp.float32)


def dot_nn(a, b):
    return jnp.dot(a, b, preferred_element_type=jnp.float32)


def split(value):
    high = value.astype(BF)
    return high, (value - high.astype(jnp.float32)).astype(BF)


MEMBERS = (((0, 1), (2, 3)), ((0, 3), (1, 2)))


def reduce_order(tiles, quarter, kind):
    result = []
    for xs in MEMBERS[kind]:
        for ys in MEMBERS[kind]:
            made = None
            for n in range(4):
                x, y = xs[n // 2], ys[n % 2]
                shift = 32 * (n - y) % 128
                moved = pltpu.roll(tiles[x], shift, 1) if shift else tiles[x]
                made = moved if made is None else jnp.where(quarter == n, moved, made)
            result.append(made)
    return jnp.concatenate(result, 1)


def density_kernel(
    cond_far, val_far, gvec_far, first_far, second_far, third_far, out,
    cond, val, gvec, prod, first, second, third, xh, xl, u, yh, yl, z, dens, sems,
):
    wide = xh.shape[1]
    chunk = GRID // CHUNKS
    loads = []
    for n in range(CHUNKS):
        lanes = pl.ds(wide * chunk * n, wide * chunk)
        loads.append(
            [
                pltpu.make_async_copy(far.at[:, lanes], near.at[:, lanes], sems.at[4 + 2 * n + m])
                for m, (far, near) in enumerate(((cond_far, cond), (val_far, val)))
            ]
        )
    far_near = ((first_far, first), (second_far, second), (third_far, third), (gvec_far, gvec))
    copies = [pltpu.make_async_copy(far, near, sems.at[n]) for n, (far, near) in enumerate(far_near)]
    for copy in sum(loads, []) + copies:
        copy.start()
    zero = jnp.zeros((32, xh.shape[1]), BF)
    for a in range(GRID):
        if a % chunk == 0:
            for load in loads[a // chunk]:
                load.wait()
        line = slice(wide * a, wide * a + wide)
        line = cond[:, line].astype(jnp.float32) * val[:, line].astype(jnp.float32)
        for tile in range(wide // 128):
            prod[tile, 4 * a : 4 * a + 4, :] = line[:, 128 * tile : 128 * tile + 128]
    for v in range(4):
        at = 128 * (v // 2) + GRID * (v % 2)
        for tile in range(wide // 128):
            high, low = split(prod[tile, pl.ds(v, GRID, stride=4), :])
            xh[at : at + GRID, 128 * tile : 128 * tile + 128] = high
            xl[at : at + GRID, 128 * tile : 128 * tile + 128] = low
    for p in range(2):
        xh[128 * p + 96 : 128 * p + 128, :] = zero
        xl[128 * p + 96 : 128 * p + 128, :] = zero
    n1 = HALF * 8
    for copy in copies:
        copy.wait()
    for pair in range(6):
        both = []
        for odd in range(2):
            start = 384 * pair + 128 * odd
            one = dot_nt(first[odd], xh[:, start : start + 256])
            two = dot_nt(first[odd, :n1], xl[:, start : start + 256])
            both.append((one[:n1] + one[n1:] + two).reshape(HALF, 8, 256))
        high, low = split(jnp.concatenate(both, 1))
        u[:, 16 * pair : 16 * pair + 16, :] = high
        u[:, 96 + 16 * pair : 96 + 16 * pair + 16, :] = low
    for start in range(0, HALF, 5):
        ks = range(start, start + 5)
        fulls = [dot_nn(second[...], u[k]) for k in ks]
        for k, full in zip(ks, fulls):
            high, low = split(full[:96] + full[96:])
            for p in range(2):
                for s in range(2):
                    rows, lanes = slice(GRID * s, GRID * s + GRID), slice(128 * p, 128 * p + 128)
                    put = (p, slice(GRID * k, GRID * k + GRID), slice(128 * s, 128 * s + 128))
                    yh[put] = high[rows, lanes]
                    yl[put] = low[rows, lanes]
    fill = yh.shape[1] - GRID * HALF
    blank = jnp.zeros((fill, 256), BF)
    for p in range(2):
        yh[p, GRID * HALF :, :] = blank
        yl[p, GRID * HALF :, :] = blank
        one = dot_nt(third[...], yh[p])
        two = dot_nt(third[:192], yl[p])
        z[192 * p : 192 * p + 192, :] = ((one[:192] + one[192:] + two) * GRID ** (-1.5)).astype(BF)
    for c in range(8):
        lanes = slice(256 * c, 256 * c + 256)
        g = gvec[:, lanes]
        plane = lax.shift_right_logical(lax.shift_right_logical(g, 4) * 43691, 17)
        k3 = g - plane * GRID
        k1 = lax.shift_right_logical(lax.shift_right_logical(plane, 4) * 43691, 17)
        k2 = plane - k1 * GRID
        flip = k3 >= HALF
        k1 = jnp.where(flip & (k1 > 0), GRID - k1, k1)
        k2 = jnp.where(flip & (k2 > 0), GRID - k2, k2)
        k3 = jnp.where(flip, GRID - k3, k3)
        spot = k3 * GRID + k2
        row = lax.broadcasted_iota(jnp.int32, (z.shape[1], 256), 0)
        hot = jnp.where(row == spot, 1.0, 0.0).astype(BF)
        t = dot_nn(z[...], hot)
        mask = lax.broadcasted_iota(jnp.int32, (GRID, 256), 0) == k1
        sign = jnp.where(flip, -1.0, 1.0)
        lines = []
        for s in range(2):
            for v in range(4):
                at = (2 * v + s) * GRID
                line = jnp.sum(jnp.where(mask, t[at : at + GRID], 0.0), 0, keepdims=True)
                lines.append(line * sign if s else line)
        dens[:, lanes] = jnp.concatenate(lines, 0)
    quarter = lax.broadcasted_iota(jnp.int32, (8, 128), 1) // 32
    for i in range(4):
        tiles = [dens[:, 512 * i + 128 * t : 512 * i + 128 * t + 128] for t in range(4)]
        orders = [reduce_order(tiles, quarter, kind) for kind in (1, 0)]
        for j in range(4):
            at = 16 * (8 * (j // 2) + 4 * (j % 2) + i)
            both = jnp.concatenate([dens[:, 512 * j : 512 * j + 512], orders[j % 2]], 0)
            out[at : at + 16, :] = both.astype(BF)


def density_call(valence, conduction, gvec_index):
    first, second, third = (jnp.asarray(t) for t in tables())
    gvec = gvec_index.reshape(1, -1)
    return pl.pallas_call(
        density_kernel,
        out_shape=jax.ShapeDtypeStruct((256, 512), BF),
        in_specs=[pl.BlockSpec(memory_space=pl.ANY)] * 6,
        out_specs=pl.BlockSpec(memory_space=pltpu.VMEM),
        scratch_shapes=[
            pltpu.VMEM(conduction.shape, BF),
            pltpu.VMEM(valence.shape, BF),
            pltpu.VMEM(gvec.shape, jnp.int32),
            pltpu.VMEM((GRID * GRID // 128, 4 * GRID, 128), jnp.float32),
            pltpu.VMEM(first.shape, BF),
            pltpu.VMEM(second.shape, BF),
            pltpu.VMEM(third.shape, BF),
            pltpu.VMEM((256, 2304), BF),
            pltpu.VMEM((256, 2304), BF),
            pltpu.VMEM((HALF, 192, 256), BF),
            pltpu.VMEM((2, 1280, 256), BF),
            pltpu.VMEM((2, 1280, 256), BF),
            pltpu.VMEM((384, 1280), BF),
            pltpu.VMEM((8, 2048), jnp.float32),
            pltpu.SemaphoreType.DMA((4 + 2 * CHUNKS,)),
        ],
        compiler_params=pltpu.CompilerParams(vmem_limit_bytes=60 * 1024 * 1024),
        cost_estimate=pl.CostEstimate(flops=5 * 10**9, bytes_accessed=3 * 10**6, transcendentals=0),
        name="density",
    )(conduction, valence, gvec, first, second, third)


def product_kernel(turn, weight, own, one, two, three, mine, first, second, third):
    blocks = (own, one, two, three)
    twice = []
    for block in blocks:
        rows = block[:, 512:640]
        parts = rows.astype(jnp.float32).reshape(16, 2, 4, 128)
        swapped = jnp.concatenate([parts[:, 1:], -parts[:, :1]], 1).reshape(128, 128)
        twice.append(jnp.concatenate([rows, swapped.astype(BF)], 1))
    lane = lax.broadcasted_iota(jnp.int32, (256, 512), 1)
    spot = ((lane // 128) ^ turn[0]) * 32 + (lane // 4) % 32 + 128 * (lane % 2)
    copies = jnp.where(lax.broadcasted_iota(jnp.int32, (256, 512), 0) == spot, 1.0, 0.0).astype(BF)
    spread = dot_nn(jnp.concatenate(twice, 0), copies)
    scale = weight[...].reshape(512, 2)
    early = (lax.broadcasted_iota(jnp.int32, (512, 512), 1) // 2) % 2 == 0
    left = (jnp.where(early, scale[:, 0:1], scale[:, 1:2]) * spread).astype(BF)
    right = jnp.concatenate([block[:, :512] for block in blocks], 0)
    total = lax.dot_general(left, right, (((0,), (0,)), ((), ())), preferred_element_type=jnp.float32)
    mine[...] = total[:128]
    first[...] = total[128:256].astype(BF)
    second[...] = total[256:384].astype(BF)
    third[...] = total[384:].astype(BF)


def product_call(turn, weight, blocks):
    piece = jax.ShapeDtypeStruct((128, 512), BF)
    vmem = pl.BlockSpec(memory_space=pltpu.VMEM)
    return pl.pallas_call(
        product_kernel,
        out_shape=(jax.ShapeDtypeStruct((128, 512), jnp.float32), piece, piece, piece),
        in_specs=[pl.BlockSpec(memory_space=pltpu.SMEM)] + [vmem] * 5,
        out_specs=(vmem,) * 4,
        compiler_params=pltpu.CompilerParams(vmem_limit_bytes=48 * 1024 * 1024),
        cost_estimate=pl.CostEstimate(flops=3 * 10**8, bytes_accessed=2 * 10**6, transcendentals=0),
        name="product",
    )(turn, weight, *blocks)


def exchange(block, step, gather):
    across, along = lax.axis_size("bx"), lax.axis_size("by")
    rest = lax.axis_size("grow") * lax.axis_size("zlo") * lax.axis_size("core")

    def partner(place, kind):
        return 3 - place if kind else place ^ 1

    pairs = []
    for x in range(across):
        for y in range(along):
            for z in range(rest):
                kind = z % 2 if gather else 1 - z % 2
                to_x = partner(x, kind) if step // 2 else x
                to_y = partner(y, kind) if step % 2 else y
                pairs.append(((x * along + y) * rest + z, (to_x * along + to_y) * rest + z))
    return lax.ppermute(block, ALL, pairs)


def on_device(valence, conduction, val_energy, cond_energy, frequencies, gvec_index, first_band):
    sent = density_call(valence, conduction, gvec_index)
    num_val = valence.shape[0]
    lines = 2 * num_val
    across = lax.axis_size("bx")
    along = lax.axis_size("by")
    group = lax.axis_size("grow") * lax.axis_size("zlo") * lax.axis_size("core")
    sent = sent.reshape(group, 2 * lines, 512)
    got = lax.all_to_all(sent, ("zlo", "core", "grow"), split_axis=0, concat_axis=0, tiled=True)
    cols = got[:, :lines].reshape(group * lines, 512)
    rows = got[:, lines:].reshape(group * lines, 512)
    x_here = lax.axis_index("bx")
    y_here = lax.axis_index("by")
    even = lax.axis_index("core") == 0

    def tile_of(place):
        return jnp.where(even, (place ^ (place >> 1)) & 1, place >> 1)

    def spot_of(place):
        return jnp.where(even, place >> 1, place & 1)

    tile = 2 * tile_of(x_here) + tile_of(y_here)
    spot = 2 * spot_of(x_here) + spot_of(y_here)
    blocks = {}
    for step in (0, 3, 2, 1):
        part = lax.dynamic_slice_in_dim(rows, (tile ^ step) * 128, 128, 1)
        block = jnp.concatenate([cols, part], 1)
        blocks[step] = exchange(block, step, True) if step else block
    steps = jnp.arange(4, dtype=jnp.int32)
    x_from = jnp.where(steps // 2 == 0, x_here, jnp.where(even, x_here ^ 1, 3 - x_here))
    y_from = jnp.where(steps % 2 == 0, y_here, jnp.where(even, y_here ^ 1, 3 - y_here))
    band = x_from * along + y_from
    chunk = jnp.arange(group, dtype=jnp.int32)
    bands = (band * group)[:, None] + chunk % 4 * 4 + chunk // 8 * 2 + chunk // 4 % 2
    energies = jnp.take(cond_energy, bands)
    gap = energies[..., None] - val_energy
    counted = bands[..., None] >= first_band
    ratio = -4.0 * gap[..., None] / (gap[..., None] ** 2 + frequencies**2)
    weight = jnp.where(counted[..., None], ratio, 0.0) / (cond_energy.shape[0] * num_val)
    weight = jnp.broadcast_to(weight[:, :, None], (across, group, 2, num_val, frequencies.shape[0]))
    weight = weight.reshape(across, group * lines, frequencies.shape[0])
    total, *pieces = product_call(spot.reshape(1), weight, [blocks[step] for step in range(4)])
    for step in (3, 2, 1):
        total = total + exchange(pieces[step - 1], step, False).astype(jnp.float32)
    return total.astype(BF).reshape(32, frequencies.shape[0], 2, 512)


def solution(mesh):
    fine = Mesh(mesh.devices.reshape(4, 4, 4, 2, 2), ALL)
    return jax.shard_map(
        on_device,
        mesh=fine,
        in_specs=(P(), P(ALL, None), P(), P(), P(), P(), P()),
        out_specs=P(("grow", "bx", "by"), None, None, ("zlo", "core")),
        check_vma=False,
    )
```

```python
import numpy as np
import jax
import jax.numpy as jnp
from jax import lax
from jax.experimental import pallas as pl
from jax.experimental.pallas import tpu as pltpu
from jax.sharding import Mesh, PartitionSpec as P
import ml_dtypes

GRID = 48
HALF = GRID // 2 + 1
BF = jnp.bfloat16
ZED = ("grow", "zlo", "core")
ALL = ("bx", "by") + ZED
CHUNKS = 4


def split_table(table):
    high = table.astype(ml_dtypes.bfloat16)
    low = (table - high.astype(np.float64)).astype(ml_dtypes.bfloat16)
    return high, low


def wave(left, right):
    angle = 2.0 * np.pi * (np.outer(left, right) % GRID) / GRID
    return np.cos(angle), np.sin(angle)


def tables():
    line = np.arange(GRID)
    cos, sin = wave(np.arange(HALF), line)
    first = np.zeros((2, HALF, 2, 4, 256))
    for odd in range(2):
        for b in range(4):
            at = 64 * odd + GRID * b
            first[odd, :, 0, b, at : at + GRID] = cos
            first[odd, :, 1, b, at : at + GRID] = -sin
    first = first.reshape(2, HALF * 8, 256)
    cos, sin = wave(line, line)
    order = np.zeros((2, GRID, 12, 2, 4))
    byb = cos.reshape(GRID, 12, 4)
    bys = sin.reshape(GRID, 12, 4)
    order[0, :, :, 0], order[0, :, :, 1] = byb, bys
    order[1, :, :, 0], order[1, :, :, 1] = -bys, byb
    second = order.reshape(2 * GRID, 2 * GRID)
    third = np.zeros((2, 2, GRID, 2, 128))
    for v in range(2):
        at = slice(GRID * v, GRID * v + GRID)
        third[v, 0, :, 0, at], third[v, 0, :, 1, at] = cos, sin
        third[v, 1, :, 0, at], third[v, 1, :, 1, at] = -sin, cos
    third = third.reshape(4 * GRID, 256)
    fh, fl = split_table(first)
    first = np.concatenate([fh, fl], 1)
    sh, sl = split_table(second)
    second = np.concatenate(
        [np.concatenate([sh, sh], 1), np.concatenate([sl, np.zeros_like(sl)], 1)], 0
    )
    th, tl = split_table(third)
    third = np.concatenate([th, tl], 0)
    return first, second, third


def dot_nt(a, b):
    return lax.dot_general(a, b, (((1,), (1,)), ((), ())), preferred_element_type=jnp.float32)


def dot_nn(a, b):
    return jnp.dot(a, b, preferred_element_type=jnp.float32)


def split(value):
    high = value.astype(BF)
    return high, (value - high.astype(jnp.float32)).astype(BF)


MEMBERS = (((0, 1), (2, 3)), ((0, 3), (1, 2)))


def reduce_order(tiles, quarter, kind):
    result = []
    for xs in MEMBERS[kind]:
        for ys in MEMBERS[kind]:
            made = None
            for n in range(4):
                x, y = xs[n // 2], ys[n % 2]
                shift = 32 * (n - y) % 128
                moved = pltpu.roll(tiles[x], shift, 1) if shift else tiles[x]
                made = moved if made is None else jnp.where(quarter == n, moved, made)
            result.append(made)
    return jnp.concatenate(result, 1)


def density_kernel(
    cond_far, val_far, gvec_far, first_far, second_far, third_far, out,
    cond, val, gvec, prod, first, second, third, xh, xl, u, yh, yl, z, dens, sems,
):
    wide = xh.shape[1]
    chunk = GRID // CHUNKS
    loads = []
    for n in range(CHUNKS):
        lanes = pl.ds(wide * chunk * n, wide * chunk)
        loads.append(
            [
                pltpu.make_async_copy(far.at[:, lanes], near.at[:, lanes], sems.at[4 + 2 * n + m])
                for m, (far, near) in enumerate(((cond_far, cond), (val_far, val)))
            ]
        )
    far_near = ((first_far, first), (second_far, second), (third_far, third), (gvec_far, gvec))
    copies = [pltpu.make_async_copy(far, near, sems.at[n]) for n, (far, near) in enumerate(far_near)]
    for copy in sum(loads, []) + copies:
        copy.start()
    zero = jnp.zeros((32, xh.shape[1]), BF)
    for a in range(GRID):
        if a % chunk == 0:
            for load in loads[a // chunk]:
                load.wait()
        line = slice(wide * a, wide * a + wide)
        line = cond[:, line].astype(jnp.float32) * val[:, line].astype(jnp.float32)
        for tile in range(wide // 128):
            prod[tile, 4 * a : 4 * a + 4, :] = line[:, 128 * tile : 128 * tile + 128]
    for v in range(4):
        at = 128 * (v // 2) + GRID * (v % 2)
        for tile in range(wide // 128):
            high, low = split(prod[tile, pl.ds(v, GRID, stride=4), :])
            xh[at : at + GRID, 128 * tile : 128 * tile + 128] = high
            xl[at : at + GRID, 128 * tile : 128 * tile + 128] = low
    for p in range(2):
        xh[128 * p + 96 : 128 * p + 128, :] = zero
        xl[128 * p + 96 : 128 * p + 128, :] = zero
    n1 = HALF * 8
    for copy in copies:
        copy.wait()
    for pair in range(6):
        both = []
        for odd in range(2):
            start = 384 * pair + 128 * odd
            one = dot_nt(first[odd], xh[:, start : start + 256])
            two = dot_nt(first[odd, :n1], xl[:, start : start + 256])
            both.append((one[:n1] + one[n1:] + two).reshape(HALF, 8, 256))
        high, low = split(jnp.concatenate(both, 1))
        u[:, 16 * pair : 16 * pair + 16, :] = high
        u[:, 96 + 16 * pair : 96 + 16 * pair + 16, :] = low
    for start in range(0, HALF, 5):
        ks = range(start, start + 5)
        fulls = [dot_nn(second[:96], u[k]) + dot_nn(second[96:, :96], u[k, :96]) for k in ks]
        for k, full in zip(ks, fulls):
            high, low = split(full)
            for p in range(2):
                for s in range(2):
                    rows, lanes = slice(GRID * s, GRID * s + GRID), slice(128 * p, 128 * p + 128)
                    put = (p, slice(GRID * k, GRID * k + GRID), slice(128 * s, 128 * s + 128))
                    yh[put] = high[rows, lanes]
                    yl[put] = low[rows, lanes]
    fill = yh.shape[1] - GRID * HALF
    blank = jnp.zeros((fill, 256), BF)
    for p in range(2):
        yh[p, GRID * HALF :, :] = blank
        yl[p, GRID * HALF :, :] = blank
        one = dot_nt(third[...], yh[p])
        two = dot_nt(third[:192], yl[p])
        z[192 * p : 192 * p + 192, :] = ((one[:192] + one[192:] + two) * GRID ** (-1.5)).astype(BF)
    for c in range(8):
        lanes = slice(256 * c, 256 * c + 256)
        g = gvec[:, lanes]
        plane = lax.shift_right_logical(lax.shift_right_logical(g, 4) * 43691, 17)
        k3 = g - plane * GRID
        k1 = lax.shift_right_logical(lax.shift_right_logical(plane, 4) * 43691, 17)
        k2 = plane - k1 * GRID
        flip = k3 >= HALF
        k1 = jnp.where(flip & (k1 > 0), GRID - k1, k1)
        k2 = jnp.where(flip & (k2 > 0), GRID - k2, k2)
        k3 = jnp.where(flip, GRID - k3, k3)
        spot = k3 * GRID + k2
        row = lax.broadcasted_iota(jnp.int32, (z.shape[1], 256), 0)
        hot = jnp.where(row == spot, 1.0, 0.0).astype(BF)
        t = dot_nn(z[...], hot)
        mask = lax.broadcasted_iota(jnp.int32, (GRID, 256), 0) == k1
        sign = jnp.where(flip, -1.0, 1.0)
        lines = []
        for s in range(2):
            for v in range(4):
                at = (2 * v + s) * GRID
                line = jnp.sum(jnp.where(mask, t[at : at + GRID], 0.0), 0, keepdims=True)
                lines.append(line * sign if s else line)
        dens[:, lanes] = jnp.concatenate(lines, 0)
    quarter = lax.broadcasted_iota(jnp.int32, (8, 128), 1) // 32
    for i in range(4):
        tiles = [dens[:, 512 * i + 128 * t : 512 * i + 128 * t + 128] for t in range(4)]
        orders = [reduce_order(tiles, quarter, kind) for kind in (1, 0)]
        for j in range(4):
            at = 16 * (8 * (j // 2) + 4 * (j % 2) + i)
            both = jnp.concatenate([dens[:, 512 * j : 512 * j + 512], orders[j % 2]], 0)
            out[at : at + 16, :] = both.astype(BF)


def density_call(valence, conduction, gvec_index):
    first, second, third = (jnp.asarray(t) for t in tables())
    gvec = gvec_index.reshape(1, -1)
    return pl.pallas_call(
        density_kernel,
        out_shape=jax.ShapeDtypeStruct((256, 512), BF),
        in_specs=[pl.BlockSpec(memory_space=pl.ANY)] * 6,
        out_specs=pl.BlockSpec(memory_space=pltpu.VMEM),
        scratch_shapes=[
            pltpu.VMEM(conduction.shape, BF),
            pltpu.VMEM(valence.shape, BF),
            pltpu.VMEM(gvec.shape, jnp.int32),
            pltpu.VMEM((GRID * GRID // 128, 4 * GRID, 128), jnp.float32),
            pltpu.VMEM(first.shape, BF),
            pltpu.VMEM(second.shape, BF),
            pltpu.VMEM(third.shape, BF),
            pltpu.VMEM((256, 2304), BF),
            pltpu.VMEM((256, 2304), BF),
            pltpu.VMEM((HALF, 192, 256), BF),
            pltpu.VMEM((2, 1280, 256), BF),
            pltpu.VMEM((2, 1280, 256), BF),
            pltpu.VMEM((384, 1280), BF),
            pltpu.VMEM((8, 2048), jnp.float32),
            pltpu.SemaphoreType.DMA((4 + 2 * CHUNKS,)),
        ],
        compiler_params=pltpu.CompilerParams(vmem_limit_bytes=60 * 1024 * 1024),
        cost_estimate=pl.CostEstimate(flops=5 * 10**9, bytes_accessed=3 * 10**6, transcendentals=0),
        name="density",
    )(conduction, valence, gvec, first, second, third)


def product_kernel(turn, weight, own, one, two, three, mine, first, second, third):
    blocks = (own, one, two, three)
    twice = []
    for block in blocks:
        rows = block[:, 512:640]
        parts = rows.astype(jnp.float32).reshape(16, 2, 4, 128)
        swapped = jnp.concatenate([parts[:, 1:], -parts[:, :1]], 1).reshape(128, 128)
        twice.append(jnp.concatenate([rows, swapped.astype(BF)], 1))
    lane = lax.broadcasted_iota(jnp.int32, (256, 512), 1)
    spot = ((lane // 128) ^ turn[0]) * 32 + (lane // 4) % 32 + 128 * (lane % 2)
    copies = jnp.where(lax.broadcasted_iota(jnp.int32, (256, 512), 0) == spot, 1.0, 0.0).astype(BF)
    spread = dot_nn(jnp.concatenate(twice, 0), copies)
    scale = weight[...].reshape(512, 2)
    early = (lax.broadcasted_iota(jnp.int32, (512, 512), 1) // 2) % 2 == 0
    left = (jnp.where(early, scale[:, 0:1], scale[:, 1:2]) * spread).astype(BF)
    right = jnp.concatenate([block[:, :512] for block in blocks], 0)
    total = lax.dot_general(left, right, (((0,), (0,)), ((), ())), preferred_element_type=jnp.float32)
    mine[...] = total[:128]
    first[...] = total[128:256].astype(BF)
    second[...] = total[256:384].astype(BF)
    third[...] = total[384:].astype(BF)


def product_call(turn, weight, blocks):
    piece = jax.ShapeDtypeStruct((128, 512), BF)
    vmem = pl.BlockSpec(memory_space=pltpu.VMEM)
    return pl.pallas_call(
        product_kernel,
        out_shape=(jax.ShapeDtypeStruct((128, 512), jnp.float32), piece, piece, piece),
        in_specs=[pl.BlockSpec(memory_space=pltpu.SMEM)] + [vmem] * 5,
        out_specs=(vmem,) * 4,
        compiler_params=pltpu.CompilerParams(vmem_limit_bytes=48 * 1024 * 1024),
        cost_estimate=pl.CostEstimate(flops=3 * 10**8, bytes_accessed=2 * 10**6, transcendentals=0),
        name="product",
    )(turn, weight, *blocks)


def exchange(block, step, gather):
    across, along = lax.axis_size("bx"), lax.axis_size("by")
    rest = lax.axis_size("grow") * lax.axis_size("zlo") * lax.axis_size("core")

    def partner(place, kind):
        return 3 - place if kind else place ^ 1

    pairs = []
    for x in range(across):
        for y in range(along):
            for z in range(rest):
                kind = z % 2 if gather else 1 - z % 2
                to_x = partner(x, kind) if step // 2 else x
                to_y = partner(y, kind) if step % 2 else y
                pairs.append(((x * along + y) * rest + z, (to_x * along + to_y) * rest + z))
    return lax.ppermute(block, ALL, pairs)


def on_device(valence, conduction, val_energy, cond_energy, frequencies, gvec_index, first_band):
    sent = density_call(valence, conduction, gvec_index)
    num_val = valence.shape[0]
    lines = 2 * num_val
    across = lax.axis_size("bx")
    along = lax.axis_size("by")
    group = lax.axis_size("grow") * lax.axis_size("zlo") * lax.axis_size("core")
    sent = sent.reshape(group, 2 * lines, 512)
    got = lax.all_to_all(sent, ("zlo", "core", "grow"), split_axis=0, concat_axis=0, tiled=True)
    cols = got[:, :lines].reshape(group * lines, 512)
    rows = got[:, lines:].reshape(group * lines, 512)
    x_here = lax.axis_index("bx")
    y_here = lax.axis_index("by")
    even = lax.axis_index("core") == 0

    def tile_of(place):
        return jnp.where(even, (place ^ (place >> 1)) & 1, place >> 1)

    def spot_of(place):
        return jnp.where(even, place >> 1, place & 1)

    tile = 2 * tile_of(x_here) + tile_of(y_here)
    spot = 2 * spot_of(x_here) + spot_of(y_here)
    blocks = {}
    for step in (0, 3, 2, 1):
        part = lax.dynamic_slice_in_dim(rows, (tile ^ step) * 128, 128, 1)
        block = jnp.concatenate([cols, part], 1)
        blocks[step] = exchange(block, step, True) if step else block
    steps = jnp.arange(4, dtype=jnp.int32)
    x_from = jnp.where(steps // 2 == 0, x_here, jnp.where(even, x_here ^ 1, 3 - x_here))
    y_from = jnp.where(steps % 2 == 0, y_here, jnp.where(even, y_here ^ 1, 3 - y_here))
    band = x_from * along + y_from
    chunk = jnp.arange(group, dtype=jnp.int32)
    bands = (band * group)[:, None] + chunk % 4 * 4 + chunk // 8 * 2 + chunk // 4 % 2
    energies = jnp.take(cond_energy, bands)
    gap = energies[..., None] - val_energy
    counted = bands[..., None] >= first_band
    ratio = -4.0 * gap[..., None] / (gap[..., None] ** 2 + frequencies**2)
    weight = jnp.where(counted[..., None], ratio, 0.0) / (cond_energy.shape[0] * num_val)
    weight = jnp.broadcast_to(weight[:, :, None], (across, group, 2, num_val, frequencies.shape[0]))
    weight = weight.reshape(across, group * lines, frequencies.shape[0])
    total, *pieces = product_call(spot.reshape(1), weight, [blocks[step] for step in range(4)])
    for step in (3, 2, 1):
        total = total + exchange(pieces[step - 1], step, False).astype(jnp.float32)
    return total.astype(BF).reshape(32, frequencies.shape[0], 2, 512)


def solution(mesh):
    fine = Mesh(mesh.devices.reshape(4, 4, 4, 2, 2), ALL)
    return jax.shard_map(
        on_device,
        mesh=fine,
        in_specs=(P(), P(ALL, None), P(), P(), P(), P(), P()),
        out_specs=P(("grow", "bx", "by"), None, None, ("zlo", "core")),
        check_vma=False,
    )
```
